256 devices in a mesh: batch: 8 (over x, core), seq: 32 (over y, z).
Axes of the slice: x: 4, y: 4, z: 8, core: 2. Of those that a mesh axis runs over, the one named last changes fastest.
Arguments:
- queries: bfloat16 [98304, 2048], P(('batch', 'seq')), parts along dimension 0, may hold values from -6 to 6
- cotangent: bfloat16 [98304, 2048], P(('batch', 'seq')), parts along dimension 0, may hold values from -6 to 6
- pool: bfloat16 [512, 128, 448], P(('batch', 'seq')), parts along dimension 0, may hold values from -6 to 6
- key_weight: bfloat16 [448, 2048], P('seq'), may hold values from -0.25 to 0.25
- value_weight: bfloat16 [448, 2048], P('seq'), may hold values from -0.25 to 0.25
- score_bias: float32 [16, 64, 256], replicated, may hold values from -300 to 300
- neighbours: int32 [1536, 2], P(('batch', 'seq')), parts along dimension 0, may hold values from 0 to 63, as said below
- place: int32 [512], P('batch'), parts along dimension 0, may hold values from 0 to 63, as said below
Outputs:
- attended: bfloat16 [98304, 2048], P(('batch', 'seq')), parts along dimension 0
- query_grad: bfloat16 [98304, 2048], P(('batch', 'seq')), parts along dimension 0
- pool_grad: float32 [512, 128, 448], P(('batch', 'seq')), parts along dimension 0
The draws below stay inside these ranges and needn't reach their ends.
There are 8 independent parts, one for each index of `batch`. The reference program is written for one: setup_inputs(seed, part) draws one part's arguments, and reference() takes and returns one part's arrays. A program takes and returns all parts, laid end to end along the dimension named above; an argument that names none is the same for every part. Nothing has to cross between parts.
Inputs may be any that keep to these rules, and one draw needn't show every extreme that they name: `neighbours`: the two blocks of a span differ. The owner of block b is place[b] // 2; among the 12 reads of one device's spans at most 1 fall on blocks of one owner, and on every device some owner gets exactly 1. `place`: A permutation of the block numbers.
All inputs are finite; a program needn't handle non-finite values.
Results may differ from the reference program's by a relative error of at most 0.015.
Values may be sent and summed in bfloat16 or wider, within the bound.
A program may use at most 128 MiB of HBM per device.

```python
import math
import jax
import jax.numpy as jnp
from jax import lax

HEADS = 16
HDIM = 128
E = 448
SPAN = 64
NB = 128
C_DEV = 6
P_DEV = 2
HD = 2048
CAP = 1
SPANS = 192
POOL = 64
N_SEQ = 32


def pool_tables(key):
    k_place, k_heat, k_noise, k_base, k_hot = jax.random.split(key, 5)
    place = jax.random.permutation(k_place, POOL).astype(jnp.int32)
    slot_width = N_SEQ * CAP
    holder = jnp.arange(slot_width, dtype=jnp.int32) // CAP
    heat = jax.random.randint(k_heat, (N_SEQ,), 0, 4)
    hottest = jax.random.randint(k_hot, (), 0, N_SEQ)
    heat = jnp.where(jnp.arange(N_SEQ) == hottest, 4, heat)
    noise = jax.random.randint(k_noise, (N_SEQ, slot_width), 0, 65536)
    ranking = (heat[holder][None, :] * 65536 + noise) * slot_width + jnp.arange(slot_width, dtype=jnp.int32)[None, :]
    chosen_vals, chosen = lax.top_k(ranking, 2 * C_DEV)
    owners = holder[chosen].reshape(SPANS, 2)
    base_row = jax.random.randint(k_base, (SPANS, 1), 0, P_DEV)
    local_row = (base_row + jnp.arange(2, dtype=jnp.int32)[None, :]) % P_DEV
    stored_at = owners * P_DEV + local_row
    logical = jnp.zeros((POOL,), jnp.int32).at[place].set(jnp.arange(POOL, dtype=jnp.int32))
    return (logical[stored_at].astype(jnp.int32), place)


def draw_neighbours(key, part):
    tables = pool_tables(key)
    return tables[0]


def draw_place(key, part):
    tables = pool_tables(key)
    return tables[1]


def draw_score_bias(key, part):
    key = jax.random.fold_in(key, 11)
    k_base = jax.random.fold_in(key, 0)
    return jnp.clip(jax.random.normal(k_base, (HEADS, SPAN, 2 * NB), jnp.float32), -4.0, 4.0)


def level_of(own_key, extent, cuts, smallest, top_value):
    gain, own = 1.0, jax.random.fold_in(own_key, 6)
    for dim, parts in cuts:
        draws = jnp.exp(jax.random.uniform(jax.random.fold_in(own, dim), (parts,), jnp.float32, smallest / len(cuts), top_value / len(cuts)))
        gain = gain * jnp.repeat(draws, extent[dim] // parts).reshape([-1 if axis == dim else 1 for axis in range(len(extent))])
    return gain


def normal_values(rng, dims, spread, reach, cuts=(), held_as=jnp.bfloat16):
    level = level_of(rng, dims, cuts, -0.22, 0.18) if cuts else 1.0
    entries = jax.random.normal(rng, dims, jnp.float32) * spread * level
    return jnp.minimum(jnp.maximum(entries, -reach), reach).astype(held_as)


def setup_inputs(seed: int = 0, part: int = 0) -> dict:
    arg_keys = jax.random.split(jax.random.key(seed), 9)
    part_splits = jax.random.split(jax.random.fold_in(arg_keys[8], part), 9)
    queries = normal_values(part_splits[0], (SPANS * SPAN, HD), 1.0, 6.0, ((0, 32),))
    cotangent = normal_values(part_splits[1], (SPANS * SPAN, HD), 1.0, 6.0, ((0, 32),))
    pool = normal_values(part_splits[2], (POOL, NB, E), 1.0, 6.0, ((0, 32),))
    key_weight = normal_values(arg_keys[3], (E, HD), E ** -0.5, 0.25, ((0, 32),))
    value_weight = normal_values(arg_keys[4], (E, HD), E ** -0.5, 0.25, ((0, 32),))
    score_bias = draw_score_bias(jax.random.fold_in(arg_keys[8], 71), part)
    neighbours = draw_neighbours(jax.random.fold_in(jax.random.fold_in(arg_keys[8], part), 71), part)
    place = draw_place(jax.random.fold_in(jax.random.fold_in(arg_keys[8], part), 71), part)
    return {"queries": queries, "cotangent": cotangent, "pool": pool, "key_weight": key_weight, "value_weight": value_weight, "score_bias": score_bias, "neighbours": neighbours, "place": place}


def span_pass(query_rows, grad_rows, gathered, key_weight, value_weight, score_bias):
    score_scale = 1.0 / math.sqrt(HDIM)
    flat_enc = gathered.reshape(2 * NB, E)
    key_rows = jnp.dot(flat_enc, key_weight, preferred_element_type=jnp.float32).astype(jnp.bfloat16)
    value_rows = jnp.dot(flat_enc, value_weight, preferred_element_type=jnp.float32).astype(jnp.bfloat16)
    query_heads = query_rows.reshape(SPAN, HEADS, HDIM).astype(jnp.float32)
    key_heads = key_rows.reshape(2 * NB, HEADS, HDIM).astype(jnp.float32)
    value_heads = value_rows.reshape(2 * NB, HEADS, HDIM).astype(jnp.float32)
    grad_heads = grad_rows.reshape(SPAN, HEADS, HDIM).astype(jnp.float32)
    scores = jnp.einsum('ihd,thd->hit', query_heads, key_heads) * score_scale + score_bias
    row_top = lax.optimization_barrier(jnp.max(scores, axis=-1, keepdims=True))
    raw_exp = jnp.exp(scores - row_top)
    attn_probs = raw_exp / lax.optimization_barrier(jnp.sum(raw_exp, axis=-1, keepdims=True))
    probs_low = lax.optimization_barrier(attn_probs.astype(jnp.bfloat16)).astype(jnp.float32)
    attended = jnp.einsum('hit,thd->ihd', probs_low, value_heads).astype(jnp.bfloat16)
    row_delta = lax.optimization_barrier(jnp.sum(grad_heads * attended.astype(jnp.float32), axis=-1))
    prob_grad = jnp.einsum('ihd,thd->hit', grad_heads, value_heads)
    score_grad = attn_probs * (prob_grad - jnp.transpose(row_delta)[:, :, None])
    dscore_low = lax.optimization_barrier(score_grad.astype(jnp.bfloat16)).astype(jnp.float32)
    query_grad = (jnp.einsum('hit,thd->ihd', dscore_low, key_heads) * score_scale).astype(jnp.bfloat16)
    key_grad = (jnp.einsum('hit,ihd->thd', dscore_low, query_heads) * score_scale).astype(jnp.bfloat16)
    value_grad = jnp.einsum('hit,ihd->thd', probs_low, grad_heads).astype(jnp.bfloat16)
    key_grad = key_grad.reshape(2 * NB, HD)
    value_grad = value_grad.reshape(2 * NB, HD)
    read_grad = jnp.dot(key_grad, key_weight.T, preferred_element_type=jnp.float32)
    read_grad = read_grad + jnp.dot(value_grad, value_weight.T, preferred_element_type=jnp.float32)
    return (attended.reshape(SPAN, HD), query_grad.reshape(SPAN, HD), read_grad.astype(jnp.bfloat16).reshape(2, NB, E))

def reference(queries, cotangent, pool, key_weight, value_weight, score_bias, neighbours, place):
    position = place[neighbours].astype(jnp.int32)
    gathered = pool[position]
    query_rows = queries.reshape(SPANS, SPAN, HD)
    grad_rows = cotangent.reshape(SPANS, SPAN, HD)

    def per_span(items):
        return span_pass(items[0], items[1], items[2], key_weight, value_weight, score_bias)
    attended, query_grad, read_grads = lax.map(per_span, (query_rows, grad_rows, gathered))
    summed = jax.ops.segment_sum(read_grads.reshape(SPANS * 2, NB * E).astype(jnp.float32), position.reshape(-1), num_segments=POOL)
    return (attended.reshape(SPANS * SPAN, HD), query_grad.reshape(SPANS * SPAN, HD), summed.reshape(POOL, NB, E))
```

```python
import functools
import math

import jax
import jax.numpy as jnp
from jax import lax
from jax.experimental import pallas as pl
from jax.experimental.pallas import tpu as pltpu
from jax.sharding import PartitionSpec as P

HEADS = 16
HDIM = 128
E = 448
SPAN = 64
NB = 128
NY = 4
NZ = 8
NX = 4
CUT = 336
REST = 448 - CUT
MIB = 1024 * 1024
MESH = pl.DeviceIdType.MESH
VM = pl.BlockSpec(memory_space=pltpu.VMEM)
SM = pl.BlockSpec(memory_space=pltpu.SMEM)


def places():
    s, b = lax.axis_index("seq"), lax.axis_index("batch")
    y, z = s // NZ, s % NZ
    x, c = b // 2, b % 2

    def at(dy, dz):
        return {"seq": ((y + dy + NY) % NY) * NZ + (z + dz + NZ) % NZ}

    dev = {
        "Y+": at(1, 0), "Y-": at(-1, 0), "YO": at(2, 0), "Z+": at(0, 1), "Z-": at(0, -1),
        "X+": {"batch": ((x + 1) % NX) * 2 + c},
        "X-": {"batch": ((x + NX - 1) % NX) * 2 + c},
        "C": {"batch": x * 2 + (1 - c)},
    }
    return y, z, x, c, dev


class Link:
    def __init__(self, dev, ssem, rsem):
        self.dev, self.ssem, self.rsem, self.all = dev, ssem, rsem, []

    def send(self, src, dst, to):
        i = len(self.all)
        cp = pltpu.make_async_remote_copy(
            src_ref=src, dst_ref=dst, send_sem=self.ssem.at[i], recv_sem=self.rsem.at[i],
            device_id=self.dev[to], device_id_type=MESH,
        )
        cp.start()
        self.all.append(cp)
        return cp

    def finish(self):
        for cp in self.all:
            cp.wait_send()


def barrier(dev, names):
    sem = pltpu.get_barrier_semaphore()
    for n in names:
        pl.semaphore_signal(sem, inc=1, device_id=dev[n], device_id_type=MESH)
    pl.semaphore_wait(sem, len(names))


def pack(x):
    tail = jnp.concatenate([x[0:64, 384:448], x[64:128, 384:448]], axis=1)
    return jnp.concatenate([x[:, 0:128], x[:, 128:256], x[:, 256:384], tail], axis=0)


def unpack(p):
    tail = jnp.concatenate([p[384:448, 0:64], p[384:448, 64:128]], axis=0)
    return jnp.concatenate([p[0:128], p[128:256], p[256:384], tail], axis=1)


N_GATHER = 124


def gather_body(asm, tab, pool, wp, r_out, wall, tabs, A, B, sbuf, relay, stab, ssem, rsem, lsem):
    y, z, x, c, dev = places()
    for j in range(2):
        pk = pack(pool[j])
        A[j] = pk[0:CUT]
        B[j] = pk[CUT:448]
    wall[0, 0, 0, 0] = wp[...]
    barrier(dev, ["Y+", "Y-", "YO", "Z+", "Z-", "X+", "X-", "C"])
    L = Link(dev, ssem, rsem)
    tcp = [
        L.send(tab, tabs.at[0], "Y+"), L.send(tab, tabs.at[1], "Y-"), L.send(tab, tabs.at[2], "YO")
    ]
    w1 = [
        L.send(wall.at[0, 0, 0, 0], wall.at[0, 0, 0, 1], "Y+"),
        L.send(wall.at[0, 0, 0, 0], wall.at[0, 0, 0, 3], "Y-"),
    ]
    b1 = [
        L.send(B.at[pl.ds(0, 2)], B.at[pl.ds(2, 2)], "Y+"),
        L.send(B.at[pl.ds(0, 2)], B.at[pl.ds(6, 2)], "Y-"),
    ]
    az = [
        L.send(A.at[pl.ds(0, 2)], A.at[pl.ds(2, 2)], "Z+"),
        L.send(A.at[pl.ds(0, 2)], A.at[pl.ds(14, 2)], "Z-"),
    ]
    for cp in w1:
        cp.wait_recv()
    w2 = [
        L.send(wall.at[0, 0, 0, 1, 0], wall.at[0, 0, 0, 2, 0], "Y+"),
        L.send(wall.at[0, 0, 0, 3, 1], wall.at[0, 0, 0, 2, 1], "Y-"),
    ]
    for cp in b1:
        cp.wait_recv()
    b2 = [
        L.send(B.at[2], B.at[4], "Y+"),
        L.send(B.at[7], B.at[5], "Y-"),
    ]
    for cp in w2:
        cp.wait_recv()
    wz = [
        L.send(wall.at[0, 0, 0], wall.at[0, 0, 1], "Z+"),
        L.send(wall.at[0, 0, 0], wall.at[0, 0, 7], "Z-"),
    ]
    core = []
    xs = {}

    def across(dz):
        xs[dz] = (
            L.send(wall.at[0, 0, dz], wall.at[1, 0, dz], "X+"),
            L.send(wall.at[0, 0, dz], wall.at[3, 0, dz], "X-"),
        )
        core.append(L.send(wall.at[0, 0, dz], wall.at[0, 1, dz], "C"))

    xf = {}

    def across_on(dz):
        for cp in xs[dz]:
            cp.wait_recv()
        if dz < 4:
            xf[dz] = L.send(wall.at[1, 0, dz], wall.at[2, 0, dz], "X+")
        else:
            xf[dz] = L.send(wall.at[3, 0, dz], wall.at[2, 0, dz], "X-")
        for k in (1, 3):
            core.append(L.send(wall.at[k, 0, dz], wall.at[k, 1, dz], "C"))

    across(0)
    for cp in tcp:
        cp.wait_recv()
    lc = [pltpu.make_async_copy(tabs.at[k], stab.at[k], lsem.at[k]) for k in range(3)]
    for cp in lc:
        cp.start()
    for cp in lc:
        cp.wait()

    direct = []
    hop = {}

    def choose(d, k, slot):
        s = stab[k, y, (z - d + NZ) % NZ]
        sbuf[slot] = lax.select(s > 0, A[2 * d + 1], A[2 * d])

    def ysend(d):
        choose(d, 1, 3 * d)
        direct.append(L.send(sbuf.at[3 * d], A.at[16 + d], "Y+"))
        choose(d, 0, 3 * d + 1)
        direct.append(L.send(sbuf.at[3 * d + 1], A.at[24 + d], "Y-"))
        choose(d, 2, 3 * d + 2)
        hop[d] = L.send(sbuf.at[3 * d + 2], relay.at[d], "Y+" if d < 4 else "Y-")

    def pass_on(d):
        hop[d].wait_recv()
        direct.append(L.send(relay.at[d], A.at[32 + d], "Y+" if d < 4 else "Y-"))

    ysend(0)
    for cp in b2:
        cp.wait_recv()
    bz = [
        L.send(B.at[pl.ds(0, 8)], B.at[pl.ds(8, 8)], "Z+"),
        L.send(B.at[pl.ds(0, 8)], B.at[pl.ds(56, 8)], "Z-"),
    ]
    for k in range(1, 4):
        m = NZ - k
        for cp in wz:
            cp.wait_recv()
        if k < 3:
            wz = [
                L.send(wall.at[0, 0, k], wall.at[0, 0, k + 1], "Z+"),
                L.send(wall.at[0, 0, m], wall.at[0, 0, m - 1], "Z-"),
            ]
        else:
            wz = [
                L.send(wall.at[0, 0, 3, pl.ds(0, 2)], wall.at[0, 0, 4, pl.ds(0, 2)], "Z+"),
                L.send(wall.at[0, 0, 5, pl.ds(2, 2)], wall.at[0, 0, 4, pl.ds(2, 2)], "Z-"),
            ]
        across(k)
        across(m)
        for cp in az:
            cp.wait_recv()
        if k < 3:
            az = [
                L.send(A.at[pl.ds(2 * k, 2)], A.at[pl.ds(2 * k + 2, 2)], "Z+"),
                L.send(A.at[pl.ds(2 * m, 2)], A.at[pl.ds(2 * m - 2, 2)], "Z-"),
            ]
        else:
            az = [L.send(A.at[6], A.at[8], "Z+"), L.send(A.at[11], A.at[9], "Z-")]
        ysend(k)
        ysend(m)
        pass_on(k - 1)
        if k > 1:
            pass_on(m + 1)
        across_on(k - 1)
        if k > 1:
            across_on(m + 1)
        for cp in bz:
            cp.wait_recv()
        if k < 3:
            bz = [
                L.send(B.at[pl.ds(8 * k, 8)], B.at[pl.ds(8 * k + 8, 8)], "Z+"),
                L.send(B.at[pl.ds(8 * m, 8)], B.at[pl.ds(8 * m - 8, 8)], "Z-"),
            ]
        else:
            bz = [
                L.send(B.at[pl.ds(24, 4)], B.at[pl.ds(32, 4)], "Z+"),
                L.send(B.at[pl.ds(44, 4)], B.at[pl.ds(36, 4)], "Z-"),
            ]
    for cp in wz:
        cp.wait_recv()
    across(4)
    for cp in az:
        cp.wait_recv()
    ysend(4)
    pass_on(3)
    pass_on(5)
    across_on(3)
    across_on(5)
    pass_on(4)
    across_on(4)
    for dz in (0, 1, 7, 2, 6, 3, 5, 4):
        xf[dz].wait_recv()
        core.append(L.send(wall.at[2, 0, dz], wall.at[2, 1, dz], "C"))
    for cp in bz:
        cp.wait_recv()
    for cp in direct:
        cp.wait_recv()
    for r in range(r_out.shape[0]):
        ia, ib = asm[r], asm[r + 16]
        r_out[r] = unpack(jnp.concatenate([A[ia], B[ib]], axis=0))
    for cp in core:
        cp.wait_recv()
    L.finish()


def gather_call(asm, tab, pool, wp, reads):
    bf = jnp.bfloat16
    return pl.pallas_call(
        gather_body,
        out_shape=(
            jax.ShapeDtypeStruct((reads, NB, E), bf),
            jax.ShapeDtypeStruct((NX, 2, NZ, NY, 2, 16, 256), bf),
            jax.ShapeDtypeStruct((3, 8, 128), jnp.int32),
        ),
        in_specs=[SM, VM, VM, VM],
        out_specs=(VM, VM, VM),
        scratch_shapes=[
            pltpu.VMEM((40, CUT, 128), bf),
            pltpu.VMEM((64, REST, 128), bf),
            pltpu.VMEM((24, CUT, 128), bf),
            pltpu.VMEM((8, CUT, 128), bf),
            pltpu.SMEM((3, 8, 128), jnp.int32),
            pltpu.SemaphoreType.DMA((N_GATHER,)),
            pltpu.SemaphoreType.DMA((N_GATHER,)),
            pltpu.SemaphoreType.DMA((3,)),
        ],
        compiler_params=pltpu.CompilerParams(
            collective_id=0, has_side_effects=True, vmem_limit_bytes=40 * MIB
        ),
        name="gather",
    )(asm, tab, pool, wp)


def nt(a, b):
    return lax.dot_general(a, b, (((1,), (1,)), ((), ())), preferred_element_type=jnp.float32)


def tn(a, b):
    return lax.dot_general(a, b, (((0,), (0,)), ((), ())), preferred_element_type=jnp.float32)


def compute_body(q, do, r, wall, bias, att, qg, rg, wk, wv, qp, op, pr, dr):
    y, z, x, c, _ = places()
    bf, f32 = jnp.bfloat16, jnp.float32
    scale = 1.0 / math.sqrt(HDIM)
    spans = r.shape[0]
    rows = spans * SPAN
    col = lax.broadcasted_iota(jnp.int32, (E, 512), 1)
    row = lax.broadcasted_iota(jnp.int32, (E, 512), 0)
    dz, dy, t = col >> 6, (col >> 4) & 3, col & 15
    source = (((y - dy) & 3) * NZ + ((z - dz) & 7)) * 14 + t
    perm = jnp.where((source == row) & (t < 14), 1.0, 0.0).astype(bf)

    def place_weight(i, _):
        dx, cc = i // 2, i % 2
        b = ((x - dx + NX) % NX) * 2 + (c + cc) % 2
        cols = pl.ds(pl.multiple_of(b * 256, 256), 256)
        for kv, w in ((0, wk), (1, wv)):
            part = wall[dx, cc, :, :, kv].reshape(512, 256)
            w[:, cols] = jnp.dot(perm, part, preferred_element_type=f32).astype(bf)
        return 0

    lax.fori_loop(0, 8, place_weight, 0)

    def project(h, _):
        cols = pl.ds(pl.multiple_of(h * HDIM, HDIM), HDIM)
        qp[:, h] = (nt(q[:, cols], wk[:, cols]) * scale).astype(bf).reshape(spans, SPAN, E)
        op[:, h] = nt(do[:, cols], wv[:, cols]).astype(bf).reshape(spans, SPAN, E)
        return 0

    lax.fori_loop(0, HEADS, project, 0)

    def span(i, _):
        rc = r[i]
        total = jnp.zeros((2 * NB, E), f32)
        for g in range(4):
            hs = pl.ds(4 * g, 4)
            qc = qp[i, hs].reshape(256, E)
            oc = op[i, hs].reshape(256, E)
            s = nt(qc, rc) + bias[hs].reshape(256, 2 * NB)
            e = jnp.exp(s - jnp.max(s, axis=-1, keepdims=True))
            p = e / jnp.sum(e, axis=-1, keepdims=True)
            low = p.astype(bf)
            pg = nt(oc, rc)
            delta = jnp.sum(low.astype(f32) * pg, axis=-1, keepdims=True)
            ds = (p * (pg - delta)).astype(bf)
            total = total + tn(ds, qc) + tn(low, oc)
            pr[i, hs] = jnp.dot(low, rc, preferred_element_type=f32).astype(bf).reshape(4, SPAN, E)
            dr[i, hs] = jnp.dot(ds, rc, preferred_element_type=f32).astype(bf).reshape(4, SPAN, E)
        low = total.astype(bf)
        rg[2 * i] = pack(low[0:NB])
        rg[2 * i + 1] = pack(low[NB:])
        return 0

    lax.fori_loop(0, spans, span, 0)
    rg[2 * spans] = jnp.zeros((448, 128), bf)

    def emit(h, _):
        cols = pl.ds(pl.multiple_of(h * HDIM, HDIM), HDIM)
        a = jnp.dot(pr[:, h].reshape(rows, E), wv[:, cols], preferred_element_type=f32)
        att[:, cols] = a.astype(bf)
        g = jnp.dot(dr[:, h].reshape(rows, E), wk[:, cols], preferred_element_type=f32)
        qg[:, cols] = (g * scale).astype(bf)
        return 0

    lax.fori_loop(0, HEADS, emit, 0)


def compute_call(q, do, r, wall, bias):
    bf = jnp.bfloat16
    spans = r.shape[0]
    stack = pltpu.VMEM((spans, HEADS, SPAN, E), bf)
    return pl.pallas_call(
        compute_body,
        out_shape=(
            jax.ShapeDtypeStruct(q.shape, bf),
            jax.ShapeDtypeStruct(q.shape, bf),
            jax.ShapeDtypeStruct((2 * spans + 1, 448, 128), bf),
        ),
        in_specs=[VM] * 5,
        out_specs=(VM, VM, VM),
        scratch_shapes=[
            pltpu.VMEM((E, HEADS * HDIM), bf), pltpu.VMEM((E, HEADS * HDIM), bf),
            stack, stack, stack, stack,
        ],
        compiler_params=pltpu.CompilerParams(vmem_limit_bytes=58 * MIB),
        name="attend",
    )(q, do, r, wall, bias)


N_RETURN = 56


def return_body(inv, tabs, rg, out, ys, yr, relay, acc, zr, D, zb, yb, ssem, rsem):
    y, z, x, c, dev = places()
    bf, f32 = jnp.bfloat16, jnp.float32
    barrier(dev, ["Y+", "Y-", "Z+", "Z-"])
    L = Link(dev, ssem, rsem)
    direct, hop = {}, {}

    def yslots(d):
        ys[3 * d] = rg[inv[8 + d], 0:CUT]
        one = L.send(ys.at[3 * d], yr.at[8 + d], "Y-")
        ys[3 * d + 1] = rg[inv[24 + d], 0:CUT]
        two = L.send(ys.at[3 * d + 1], yr.at[d], "Y+")
        ys[3 * d + 2] = rg[inv[16 + d], 0:CUT]
        hop[d] = L.send(ys.at[3 * d + 2], relay.at[d], "Y-" if d < 4 else "Y+")
        direct[d] = [one, two]

    def pass_on(d):
        hop[d].wait_recv()
        direct[d].append(L.send(relay.at[d], yr.at[16 + d], "Y-" if d < 4 else "Y+"))

    def dense(dz):
        for dy in range(NY):
            k = dy * NZ + dz
            v = rg[inv[k], CUT:448]
            s = inv[32 + k]
            zero = jnp.zeros_like(v)
            D[dz * 8 + dy * 2] = lax.select(s > 0, zero, v)
            D[dz * 8 + dy * 2 + 1] = lax.select(s > 0, v, zero)

    def row_sum(d):
        for cp in direct[d]:
            cp.wait_recv()
        zp = (z - d + NZ) % NZ
        terms = [(rg[inv[d], 0:CUT], inv[32 + d])]
        for k in range(3):
            terms.append((yr[8 * k + d], tabs[k, y, zp]))
        sums = []
        for j in range(2):
            t = None
            for v, s in terms:
                v = v.astype(f32)
                zero = jnp.zeros_like(v)
                v = lax.select(s > 0, v, zero) if j else lax.select(s > 0, zero, v)
                t = v if t is None else t + v
            sums.append(t)
        return sums

    def add_to(ref, i, n, src, k):
        for a in range(n):
            ref[i + a] = (ref[i + a].astype(f32) + src[k + a].astype(f32)).astype(bf)

    yslots(4)
    dense(4)
    bz = [
        L.send(D.at[pl.ds(32, 4)], zb.at[pl.ds(0, 4)], "Z-"),
        L.send(D.at[pl.ds(36, 4)], zb.at[pl.ds(28, 4)], "Z+"),
    ]
    yslots(3)
    yslots(5)
    dense(3)
    dense(5)
    for d in (2, 6, 1, 7, 0):
        yslots(d)
    for d in (2, 6, 1, 7, 0):
        dense(d)
    pass_on(4)
    az = []
    for k in range(3, -1, -1):
        m = NZ - k
        for cp in bz:
            cp.wait_recv()
        if k == 3:
            add_to(D, 24, 4, zb, 0)
            add_to(D, 44, 4, zb, 28)
        elif k > 0:
            add_to(D, 8 * k, 8, zb, 4 + 8 * (2 - k))
            add_to(D, 8 * m, 8, zb, 32 + 8 * (2 - k))
        if k > 0:
            at = 4 + 8 * (3 - k)
            bz = [
                L.send(D.at[pl.ds(8 * k, 8)], zb.at[pl.ds(at, 8)], "Z-"),
                L.send(D.at[pl.ds(8 * m, 8)], zb.at[pl.ds(28 + at, 8)], "Z+"),
            ]
        else:
            for a in range(8):
                t = D[a].astype(f32) + zb[20 + a].astype(f32) + zb[48 + a].astype(f32)
                D[a] = t.astype(bf)
            by = [L.send(D.at[4], yb.at[0], "Y-"), L.send(D.at[5], yb.at[3], "Y+")]
        e = k + 1
        if e == 4:
            s0, s1 = row_sum(4)
            acc[8] = s0.astype(bf)
            acc[9] = s1.astype(bf)
            az = [L.send(acc.at[8], zr.at[0], "Z-"), L.send(acc.at[9], zr.at[7], "Z+")]
        else:
            sums = {d: row_sum(d) for d in (e, NZ - e)}
            for cp in az:
                cp.wait_recv()
            at = 1 + 2 * (3 - e)
            for d, base in ((e, 0), (NZ - e, 7)):
                s0, s1 = sums[d]
                if e == 3:
                    if base == 0:
                        s0 = s0 + zr[0].astype(f32)
                    else:
                        s1 = s1 + zr[7].astype(f32)
                else:
                    s0 = s0 + zr[base + at - 2].astype(f32)
                    s1 = s1 + zr[base + at - 1].astype(f32)
                acc[2 * d] = s0.astype(bf)
                acc[2 * d + 1] = s1.astype(bf)
            f = NZ - e
            az = [
                L.send(acc.at[pl.ds(2 * e, 2)], zr.at[pl.ds(at, 2)], "Z-"),
                L.send(acc.at[pl.ds(2 * f, 2)], zr.at[pl.ds(7 + at, 2)], "Z+"),
            ]
        pass_on(k)
        if k > 0:
            pass_on(m)
    for cp in by:
        cp.wait_recv()
    add_to(D, 2, 1, yb, 0)
    add_to(D, 7, 1, yb, 3)
    by = [
        L.send(D.at[pl.ds(2, 2)], yb.at[pl.ds(1, 2)], "Y-"),
        L.send(D.at[pl.ds(6, 2)], yb.at[pl.ds(4, 2)], "Y+"),
    ]
    home = row_sum(0)
    for cp in az:
        cp.wait_recv()
    for cp in by:
        cp.wait_recv()
    for j in range(2):
        a = home[j] + zr[5 + j].astype(f32) + zr[12 + j].astype(f32)
        b = D[j].astype(f32) + yb[1 + j].astype(f32) + yb[4 + j].astype(f32)
        out[j] = unpack(jnp.concatenate([a, b], axis=0))
    L.finish()


def return_call(inv, tabs, rg):
    bf = jnp.bfloat16
    return pl.pallas_call(
        return_body,
        out_shape=jax.ShapeDtypeStruct((2, NB, E), jnp.float32),
        in_specs=[SM, SM, VM],
        out_specs=VM,
        scratch_shapes=[
            pltpu.VMEM((24, CUT, 128), bf),
            pltpu.VMEM((24, CUT, 128), bf),
            pltpu.VMEM((8, CUT, 128), bf),
            pltpu.VMEM((16, CUT, 128), bf),
            pltpu.VMEM((14, CUT, 128), bf),
            pltpu.VMEM((64, REST, 128), bf),
            pltpu.VMEM((56, REST, 128), bf),
            pltpu.VMEM((6, REST, 128), bf),
            pltpu.SemaphoreType.DMA((N_RETURN,)),
            pltpu.SemaphoreType.DMA((N_RETURN,)),
        ],
        compiler_params=pltpu.CompilerParams(
            collective_id=1, has_side_effects=True, vmem_limit_bytes=40 * MIB
        ),
        name="giveback",
    )(inv, tabs, rg)


def tables(neighbours, place):
    s = lax.axis_index("seq")
    y, z = s // NZ, s % NZ
    reads = neighbours.size
    pos = place[neighbours].reshape(reads)
    owner, j = pos // 2, pos % 2
    dy, dz = (y - owner // NZ) % NY, (z - owner % NZ) % NZ
    ia = jnp.where(dy == 0, 2 * dz + j, jnp.where(dy == 1, 16, jnp.where(dy == 3, 24, 32)) + dz)
    ib = dz * 8 + dy * 2 + j
    gap = jnp.zeros((16 - reads,), jnp.int32)
    asm = jnp.concatenate([ia, gap, ib, gap])
    own = jnp.arange(8)[:, None] * NZ + jnp.arange(128)[None, :]
    real = jnp.arange(128)[None, :] < NZ
    tab = jnp.sum(
        jnp.where((own[None] == owner[:, None, None]) & real[None], j[:, None, None], 0), axis=0
    )
    hit = (dy * NZ + dz)[:, None] == jnp.arange(32)[None, :]
    which = jnp.min(jnp.where(hit, jnp.arange(reads)[:, None], reads), axis=0)
    pick = jnp.max(jnp.where(hit, j[:, None], 0), axis=0)
    inv = jnp.concatenate([which, pick]).astype(jnp.int32)
    return asm.astype(jnp.int32), tab.astype(jnp.int32), inv


def on_device(queries, cotangent, pool, key_weight, value_weight, score_bias, neighbours, place):
    spans = queries.shape[0] // SPAN
    asm, tab, inv = tables(neighbours, place)
    b = lax.axis_index("batch")
    wp = jnp.stack([key_weight, value_weight])
    wp = lax.dynamic_slice(wp, (0, 0, b * 256), (2, 14, 256))
    wp = jnp.pad(wp, ((0, 0), (0, 2), (0, 0)))
    r, wall, tabs = gather_call(asm, tab, pool, wp, 2 * spans)
    att, qg, rg = compute_call(
        queries, cotangent, r.reshape(spans, 2 * NB, E), wall, score_bias
    )
    return att, qg, return_call(inv, tabs, rg)


def solution(mesh):
    both = ("batch", "seq")
    in_specs = (
        P(both, None), P(both, None), P(both, None, None), P("seq", None), P("seq", None),
        P(), P(both, None), P("batch"),
    )
    out_specs = (P(both, None), P(both, None), P(both, None, None))
    return jax.shard_map(
        on_device, mesh=mesh, in_specs=in_specs, out_specs=out_specs, check_vma=False
    )
```

```python
import functools
import math

import jax
import jax.numpy as jnp
from jax import lax
from jax.experimental import pallas as pl
from jax.experimental.pallas import tpu as pltpu
from jax.sharding import PartitionSpec as P

HEADS = 16
HDIM = 128
E = 448
SPAN = 64
NB = 128
NY = 4
NZ = 8
NX = 4
LOW = 240
TOP = 448 - LOW
LOW2 = 304
TOP2 = 448 - LOW2
MIB = 1024 * 1024
VMEM_ASK = 63 * MIB
MESH = pl.DeviceIdType.MESH
VM = pl.BlockSpec(memory_space=pltpu.VMEM)
SM = pl.BlockSpec(memory_space=pltpu.SMEM)


def places():
    s, b = lax.axis_index("seq"), lax.axis_index("batch")
    y, z = s // NZ, s % NZ
    x, c = b // 2, b % 2

    def at(dy, dz):
        return {"seq": ((y + dy + NY) % NY) * NZ + (z + dz + NZ) % NZ}

    dev = {
        "Y+": at(1, 0), "Y-": at(-1, 0), "YO": at(2, 0), "Z+": at(0, 1), "Z-": at(0, -1),
        "X+": {"batch": ((x + 1) % NX) * 2 + c},
        "X-": {"batch": ((x + NX - 1) % NX) * 2 + c},
        "C": {"batch": x * 2 + (1 - c)},
    }
    return y, z, x, c, dev


class Link:
    def __init__(self, dev, ssem, rsem):
        self.dev, self.ssem, self.rsem, self.n, self.all = dev, ssem, rsem, 0, []

    def send(self, src, dst, to):
        i, self.n = self.n, self.n + 1
        cp = pltpu.make_async_remote_copy(
            src_ref=src, dst_ref=dst, send_sem=self.ssem.at[i], recv_sem=self.rsem.at[i],
            device_id=self.dev[to], device_id_type=MESH,
        )
        cp.start()
        self.all.append(cp)
        return cp

    def finish(self):
        for cp in self.all:
            cp.wait_send()
        self.all = []


def barrier(dev, names):
    sem = pltpu.get_barrier_semaphore()
    for n in names:
        pl.semaphore_signal(sem, inc=1, device_id=dev[n], device_id_type=MESH)
    pl.semaphore_wait(sem, len(names))


def pack(x):
    tail = jnp.concatenate([x[0:64, 384:448], x[64:128, 384:448]], axis=1)
    return jnp.concatenate([x[:, 0:128], x[:, 128:256], x[:, 256:384], tail], axis=0)


def unpack(p):
    tail = jnp.concatenate([p[384:448, 0:64], p[384:448, 64:128]], axis=0)
    return jnp.concatenate([p[0:128], p[128:256], p[256:384], tail], axis=1)


def nt(a, b):
    return lax.dot_general(a, b, (((1,), (1,)), ((), ())), preferred_element_type=jnp.float32)


def tn(a, b):
    return lax.dot_general(a, b, (((0,), (0,)), ((), ())), preferred_element_type=jnp.float32)


N_COPIES = 168


def body(asm, inv, tab, pool, wp, q_hbm, do_hbm, bias_hbm, att_hbm, qg_hbm, out,
         q, do, bias, bias_t, wall, perm, wk, wv, qo, pp, r, tabs, stab, F, O, sb, sbo, rg,
         yr, yro, yso, acc, oc, zr, zo, of, ssem, rsem, lsem):
    y, z, x, c, dev = places()
    bf, f32 = jnp.bfloat16, jnp.float32
    scale = 1.0 / math.sqrt(HDIM)
    spans = r.shape[0]
    rows = spans * SPAN
    loads = [
        pltpu.make_async_copy(a, b, lsem.at[i])
        for i, (a, b) in enumerate(((bias_hbm, bias), (q_hbm, q), (do_hbm, do)))
    ]
    for cp in loads:
        cp.start()
    for j in range(2):
        F[j] = pack(pool[j])
    wall[0, 0, 0, 0] = wp[...]
    barrier(dev, ["Y+", "Y-", "YO", "Z+", "Z-", "X+", "X-", "C"])
    L = Link(dev, ssem, rsem)

    def got(cps):
        for cp in cps:
            cp.wait_recv()

    tcp = [
        L.send(tab, tabs.at[0], "Y+"), L.send(tab, tabs.at[1], "Y-"), L.send(tab, tabs.at[2], "YO")
    ]
    w1 = [
        L.send(wall.at[0, 0, 0, 0], wall.at[0, 0, 0, 1], "Y+"),
        L.send(wall.at[0, 0, 0, 0], wall.at[0, 0, 0, 3], "Y-"),
        L.send(wall.at[0, 0, 0, 0], wall.at[0, 0, 0, 2], "YO"),
    ]

    def own(k, j):
        a, b = k - 1, (NZ - k + 1) % NZ
        cps = []
        if k < 4 or j == 0:
            cps.append(L.send(F.at[2 * a + j], F.at[2 * k + j], "Z+"))
        if k < 4 or j == 1:
            cps.append(L.send(F.at[2 * b + j], F.at[2 * (NZ - k) + j], "Z-"))
        return cps

    def opp(k):
        a, b, m = k - 1, (NZ - k + 1) % NZ, NZ - k
        if k == 4:
            return [L.send(O.at[6], O.at[8], "Z+"), L.send(O.at[11], O.at[9], "Z-")]
        return [
            L.send(O.at[pl.ds(2 * a, 2)], O.at[pl.ds(2 * k, 2)], "Z+"),
            L.send(O.at[pl.ds(2 * b, 2)], O.at[pl.ds(2 * m, 2)], "Z-"),
        ]

    def weights(k):
        a, b, m = k - 1, (NZ - k + 1) % NZ, NZ - k
        if k == 4:
            return [
                L.send(wall.at[0, 0, 3, pl.ds(0, 2)], wall.at[0, 0, 4, pl.ds(0, 2)], "Z+"),
                L.send(wall.at[0, 0, 5, pl.ds(2, 2)], wall.at[0, 0, 4, pl.ds(2, 2)], "Z-"),
            ]
        return [
            L.send(wall.at[0, 0, a], wall.at[0, 0, k], "Z+"),
            L.send(wall.at[0, 0, b], wall.at[0, 0, m], "Z-"),
        ]

    core, xs, xf = {}, {}, {}

    def to_core(dx, dz):
        core[dx, dz] = L.send(wall.at[dx, 0, dz], wall.at[dx, 1, dz], "C")

    def across(dz):
        xs[dz] = (
            L.send(wall.at[0, 0, dz], wall.at[1, 0, dz], "X+"),
            L.send(wall.at[0, 0, dz], wall.at[3, 0, dz], "X-"),
        )
        to_core(0, dz)

    def across_on(dz):
        got(xs[dz])
        if dz < 4:
            xf[dz] = L.send(wall.at[1, 0, dz], wall.at[2, 0, dz], "X+")
        else:
            xf[dz] = L.send(wall.at[3, 0, dz], wall.at[2, 0, dz], "X-")
        to_core(1, dz)
        to_core(3, dz)

    direct = []

    def ysend(d):
        zp = (z - d + NZ) % NZ
        sb[2 * d] = lax.select(stab[1, y, zp] > 0, F[2 * d + 1], F[2 * d])
        direct.append(L.send(sb.at[2 * d], F.at[16 + d], "Y+"))
        sb[2 * d + 1] = lax.select(stab[0, y, zp] > 0, F[2 * d + 1], F[2 * d])
        direct.append(L.send(sb.at[2 * d + 1], F.at[24 + d], "Y-"))
        sbo[d] = lax.select(stab[2, y, zp] > 0, F[2 * d + 1, 0:TOP], F[2 * d, 0:TOP])
        direct.append(L.send(sbo.at[d], F.at[32 + d, pl.ds(0, TOP)], "YO"))

    def project(dx, cc):
        if cc:
            got([core[dx, dz] for dz in range(NZ)])
        b = ((x - dx + NX) % NX) * 2 + (c + cc) % 2
        wide = pl.ds(pl.multiple_of(b * 256, 256), 256)
        pm = perm[...]
        for kv, w, src, base in ((0, wk, q, 0), (1, wv, do, HEADS * SPAN)):
            part = wall[dx, cc, :, :, kv].reshape(512, 256)
            wb = jnp.dot(pm, part, preferred_element_type=f32).astype(bf)
            w[:, wide] = wb
            rows_in = src[:, wide]
            for hh in range(2):
                t = nt(rows_in[:, hh * HDIM:(hh + 1) * HDIM], wb[:, hh * HDIM:(hh + 1) * HDIM])
                if kv == 0:
                    t = t * scale
                at = pl.ds(pl.multiple_of(base + b * 128 + hh * SPAN, SPAN), SPAN)
                qo[:, at] = t.astype(bf).reshape(spans, SPAN, E)

    o1 = [own(1, 0)]
    ex = L.send(F.at[pl.ds(0, 2), pl.ds(TOP, LOW)], O.at[pl.ds(0, 2)], "YO")
    got(w1)
    wz = weights(1)
    o1.append(own(1, 1))
    across(0)
    got(tcp)
    lc = [pltpu.make_async_copy(tabs.at[k], stab.at[k], lsem.at[3 + k]) for k in range(3)]
    for cp in lc:
        cp.start()
    for cp in lc:
        cp.wait()
    ysend(0)
    col = lax.broadcasted_iota(jnp.int32, (E, 512), 1)
    row = lax.broadcasted_iota(jnp.int32, (E, 512), 0)
    dz, dy, t = col >> 6, (col >> 4) & 3, col & 15
    source = (((y - dy) & 3) * NZ + ((z - dz) & 7)) * 14 + t
    perm[...] = jnp.where((source == row) & (t < 14), 1.0, 0.0).astype(bf)
    got(o1[0])
    o2 = [own(2, 0)]
    got(wz)
    wz = weights(2)
    across(1)
    across(7)
    got(o1[1])
    o2.append(own(2, 1))
    ysend(1)
    ysend(7)
    got([ex])
    oz = opp(1)
    got(wz)
    wz = weights(3)
    across(2)
    across(6)
    across_on(0)
    loads[0].wait()
    bias_t[...] = bias[...].T
    got(o2[0])
    o3 = [own(3, 0)]
    got(wz)
    wz = weights(4)
    across(3)
    across(5)
    got(o2[1])
    o3.append(own(3, 1))
    ysend(2)
    ysend(6)
    across_on(1)
    across_on(7)
    got(oz)
    oz = opp(2)
    got(wz)
    across(4)
    across_on(2)
    across_on(6)
    loads[1].wait()
    loads[2].wait()
    project(0, 0)
    got(o3[0])
    o4 = own(4, 0)
    got(o3[1])
    o4 = o4 + own(4, 1)
    ysend(3)
    ysend(5)
    across_on(3)
    across_on(5)
    got(oz)
    oz = opp(3)
    across_on(4)
    project(0, 1)
    project(1, 0)
    got(o4)
    ysend(4)
    for d in range(NZ):
        xf[d].wait_recv()
        to_core(2, d)
    project(3, 0)
    got(oz)
    oz = opp(4)
    project(1, 1)
    project(3, 1)
    project(2, 0)
    project(2, 1)
    got(oz)
    got(direct)
    for d in range(NZ):
        F[32 + d, TOP:448] = lax.select(inv[48 + d] > 0, O[2 * d + 1], O[2 * d])
    for i in range(spans):
        for j in range(2):
            r[i, j * NB:(j + 1) * NB] = unpack(F[asm[2 * i + j]])
    L.finish()

    half = HEADS * SPAN

    def stage1(i):
        return nt(r[i], qo[i, 0:half]) + bias_t[...], nt(r[i], qo[i, half:])

    def stage2(i, s, pg):
        e = jnp.exp(s - jnp.max(s, axis=0, keepdims=True))
        p = e * (1.0 / jnp.sum(e, axis=0, keepdims=True))
        low = p.astype(bf)
        delta = jnp.sum(low.astype(f32) * pg, axis=0, keepdims=True)
        ds = (p * (pg - delta)).astype(bf)
        pp[i, :, 0:half] = ds
        pp[i, :, half:] = low
        return ds, low

    def stage3(i, ds, low):
        g = jnp.dot(ds, qo[i, 0:half], preferred_element_type=f32)
        g = (g + jnp.dot(low, qo[i, half:], preferred_element_type=f32)).astype(bf)
        rg[2 * i] = pack(g[0:NB])
        rg[2 * i + 1] = pack(g[NB:])

    ahead, behind = stage1(0), None
    for i in range(spans):
        later = stage1(i + 1) if i + 1 < spans else None
        now = stage2(i, *ahead)
        if behind is not None:
            stage3(i - 1, *behind)
        ahead, behind = later, now
    stage3(spans - 1, *behind)
    rg[2 * spans] = jnp.zeros((448, 128), bf)

    back = {}

    def yslots(d):
        sb[2 * d] = rg[inv[8 + d]]
        one = L.send(sb.at[2 * d], yr.at[8 + d], "Y-")
        sb[2 * d + 1] = rg[inv[24 + d]]
        two = L.send(sb.at[2 * d + 1], yr.at[d], "Y+")
        yso[d] = rg[inv[16 + d], 0:TOP2]
        back[d] = [one, two, L.send(yso.at[d], yro.at[d], "YO")]

    def dense(d):
        v = rg[inv[16 + d], TOP2:448]
        s = inv[48 + d]
        zero = jnp.zeros_like(v)
        oc[2 * d] = lax.select(s > 0, zero, v)
        oc[2 * d + 1] = lax.select(s > 0, v, zero)

    def pick(terms, j):
        t = None
        for v, s in terms:
            v = v.astype(f32)
            zero = jnp.zeros_like(v)
            v = lax.select(s > 0, v, zero) if j else lax.select(s > 0, zero, v)
            t = v if t is None else t + v
        return t

    def row_sum(d, j):
        zp = (z - d + NZ) % NZ
        s0, s1, s2 = tabs_at(0, zp), tabs_at(1, zp), tabs_at(2, zp)
        mine = rg[inv[d]]
        near = [(mine, inv[32 + d]), (yr[d], s0), (yr[8 + d], s1)]
        top = [(v[0:TOP2], s) for v, s in near] + [(yro[d], s2)]
        return pick(top, j), pick([(v[TOP2:448], s) for v, s in near], j)

    def tabs_at(k, zp):
        return stab[k, y, zp]

    def add_block(d, j, extra):
        top, low = row_sum(d, j)
        for ref in extra:
            top = top + ref[0:TOP2].astype(f32)
            low = low + ref[TOP2:448].astype(f32)
        return top, low

    group = 4 * SPAN
    outs = []

    def mix(g, base):
        for i in range(spans):
            t = tn(pp[i, :, base + g * group:base + (g + 1) * group], r[i])
            qo[i, base + g * group:base + (g + 1) * group] = t.astype(bf)

    def emit(g, base, w, dst, hbm, k):
        for h in range(4 * g, 4 * g + 4):
            v = qo[:, base + h * SPAN:base + (h + 1) * SPAN].reshape(rows, E)
            t = jnp.dot(v, w[:, h * HDIM:(h + 1) * HDIM], preferred_element_type=f32)
            if k == 1:
                t = t * scale
            dst[:, h * HDIM:(h + 1) * HDIM] = t.astype(bf)
        cols = pl.ds(4 * g * HDIM, 4 * HDIM)
        cp = pltpu.make_async_copy(dst.at[:, cols], hbm.at[:, cols], lsem.at[6 + 2 * g + k])
        cp.start()
        outs.append(cp)

    tasks = []
    for g in range(4):
        tasks.append(functools.partial(mix, g, half))
        tasks.append(functools.partial(emit, g, half, wv, q, att_hbm, 0))
        tasks.append(functools.partial(mix, g, 0))
        tasks.append(functools.partial(emit, g, 0, wk, do, qg_hbm, 1))

    def work(n):
        for _ in range(n):
            if tasks:
                tasks.pop(0)()

    def add_to(ref, i, n, src, k):
        for a in range(n):
            ref[i + a] = (ref[i + a].astype(f32) + src[k + a].astype(f32)).astype(bf)

    yslots(4)
    dense(4)
    oz = [L.send(oc.at[8], zo.at[0], "Z-"), L.send(oc.at[9], zo.at[7], "Z+")]
    yslots(3)
    yslots(5)
    dense(3)
    dense(5)
    yslots(2)
    yslots(6)
    yslots(1)
    yslots(7)
    yslots(0)
    for d in (2, 6, 1, 7, 0):
        dense(d)

    def own_back(e, prev):
        if e == 4:
            got(back[4])
            cps = []
            for j, to, at in ((0, "Z-", 0), (1, "Z+", 7)):
                top, low = row_sum(4, j)
                acc[8 + j, 0:TOP2] = top.astype(bf)
                acc[8 + j, TOP2:448] = low.astype(bf)
                cps.append(L.send(acc.at[8 + j], zr.at[at], to))
            return cps
        f = NZ - e
        got(back[e])
        got(back[f])
        at = 1 + 2 * (3 - e)
        cps = []
        for j in range(2):
            for d, base, to in ((e, 0, "Z-"), (f, 7, "Z+")):
                extra = []
                if e == 3:
                    if (j == 0) == (base == 0):
                        prev[base // 7].wait_recv()
                        extra = [zr.at[base]]
                else:
                    prev[2 * j + base // 7].wait_recv()
                    extra = [zr.at[base + at - 2 + j]]
                top, low = add_block(d, j, extra)
                acc[2 * d + j, 0:TOP2] = top.astype(bf)
                acc[2 * d + j, TOP2:448] = low.astype(bf)
                cps.append(L.send(acc.at[2 * d + j], zr.at[base + at + j], to))
        return cps

    def opp_back(e):
        got(oz)
        f = NZ - e
        if e == 3:
            add_to(oc, 6, 1, zo, 0)
            add_to(oc, 11, 1, zo, 7)
        elif e > 0:
            add_to(oc, 2 * e, 2, zo, 1 + 2 * (2 - e))
            add_to(oc, 2 * f, 2, zo, 8 + 2 * (2 - e))
        else:
            for j in range(2):
                t = oc[j].astype(f32) + zo[5 + j].astype(f32) + zo[12 + j].astype(f32)
                oc[j] = t.astype(bf)
            return [L.send(oc.at[pl.ds(0, 2)], of, "YO")]
        at = 1 + 2 * (3 - e)
        return [
            L.send(oc.at[pl.ds(2 * e, 2)], zo.at[pl.ds(at, 2)], "Z-"),
            L.send(oc.at[pl.ds(2 * f, 2)], zo.at[pl.ds(7 + at, 2)], "Z+"),
        ]

    work(1)
    oz = opp_back(3)
    work(1)
    oy = own_back(4, None)
    work(2)
    oz = opp_back(2)
    work(2)
    oy = own_back(3, oy)
    work(2)
    oz = opp_back(1)
    work(3)
    oy = own_back(2, oy)
    work(2)
    oz = opp_back(0)
    work(2)
    oy = own_back(1, oy)
    work(16)
    got(back[0])
    for j in range(2):
        got(oy[2 * j:2 * j + 2])
        if j == 0:
            got(oz)
        top, low = add_block(0, j, [zr.at[5 + j], zr.at[12 + j]])
        low = low + of[j].astype(f32)
        out[j] = unpack(jnp.concatenate([top, low], axis=0))
    for cp in outs:
        cp.wait()
    L.finish()


def call(asm, inv, tab, pool, wp, q, do, bias):
    bf, f32 = jnp.bfloat16, jnp.float32
    rows = q.shape[0]
    spans = rows // SPAN
    sizes = (
        ((rows, 2048), bf), ((rows, 2048), bf),
        ((HEADS * SPAN, 256), f32), ((256, HEADS * SPAN), f32),
        ((NX, 2, NZ, NY, 2, 16, 256), bf), ((E, 512), bf),
        ((E, 2048), bf), ((E, 2048), bf),
        ((spans, 2 * HEADS * SPAN, E), bf), ((spans, 256, 2 * HEADS * SPAN), bf),
        ((spans, 256, E), bf), ((3, 8, 128), jnp.int32), None,
        ((40, 448, 128), bf), ((16, LOW, 128), bf),
        ((16, 448, 128), bf), ((8, TOP, 128), bf), ((2 * spans + 1, 448, 128), bf),
        ((16, 448, 128), bf), ((8, TOP2, 128), bf), ((8, TOP2, 128), bf),
        ((16, 448, 128), bf), ((16, LOW2, 128), bf),
        ((14, 448, 128), bf), ((14, LOW2, 128), bf), ((2, LOW2, 128), bf),
    )
    scratch = [
        pltpu.SMEM((3, 8, 128), jnp.int32) if s is None else pltpu.VMEM(*s) for s in sizes
    ]
    scratch += [
        pltpu.SemaphoreType.DMA((N_COPIES,)), pltpu.SemaphoreType.DMA((N_COPIES,)),
        pltpu.SemaphoreType.DMA((14,)),
    ]
    hbm = pl.BlockSpec(memory_space=pl.ANY)
    return pl.pallas_call(
        body,
        out_shape=(
            jax.ShapeDtypeStruct(q.shape, bf),
            jax.ShapeDtypeStruct(q.shape, bf),
            jax.ShapeDtypeStruct((2, NB, E), f32),
        ),
        in_specs=[SM, SM, VM, VM, VM, hbm, hbm, hbm],
        out_specs=(hbm, hbm, VM),
        scratch_shapes=scratch,
        compiler_params=pltpu.CompilerParams(
            collective_id=0, has_side_effects=True, vmem_limit_bytes=VMEM_ASK
        ),
        name="retro",
    )(asm, inv, tab, pool, wp, q, do, bias)


def tables(neighbours, place):
    s = lax.axis_index("seq")
    y, z = s // NZ, s % NZ
    reads = neighbours.size
    pos = place[neighbours].reshape(reads)
    owner, j = pos // 2, pos % 2
    dy, dz = (y - owner // NZ) % NY, (z - owner % NZ) % NZ
    ia = jnp.where(dy == 0, 2 * dz + j, jnp.where(dy == 1, 16, jnp.where(dy == 3, 24, 32)) + dz)
    gap = jnp.zeros((16 - reads,), jnp.int32)
    asm = jnp.concatenate([ia, gap])
    own = jnp.arange(8)[:, None] * NZ + jnp.arange(128)[None, :]
    real = jnp.arange(128)[None, :] < NZ
    tab = jnp.sum(
        jnp.where((own[None] == owner[:, None, None]) & real[None], j[:, None, None], 0), axis=0
    )
    hit = (dy * NZ + dz)[:, None] == jnp.arange(32)[None, :]
    which = jnp.min(jnp.where(hit, jnp.arange(reads)[:, None], reads), axis=0)
    pick = jnp.max(jnp.where(hit, j[:, None], 0), axis=0)
    inv = jnp.concatenate([which, pick]).astype(jnp.int32)
    return asm.astype(jnp.int32), tab.astype(jnp.int32), inv


def on_device(queries, cotangent, pool, key_weight, value_weight, score_bias, neighbours, place):
    asm, tab, inv = tables(neighbours, place)
    b = lax.axis_index("batch")
    wp = jnp.stack([key_weight, value_weight])
    wp = lax.dynamic_slice(wp, (0, 0, b * 256), (2, 14, 256))
    wp = jnp.pad(wp, ((0, 0), (0, 2), (0, 0)))
    bias = score_bias.reshape(HEADS * SPAN, 2 * NB)
    return call(asm, inv, tab, pool, wp, queries, cotangent, bias)


def solution(mesh):
    both = ("batch", "seq")
    in_specs = (
        P(both, None), P(both, None), P(both, None, None), P("seq", None), P("seq", None),
        P(), P(both, None), P("batch"),
    )
    out_specs = (P(both, None), P(both, None), P(both, None, None))
    return jax.shard_map(
        on_device, mesh=mesh, in_specs=in_specs, out_specs=out_specs, check_vma=False
    )
```

```python
import functools
import math

import jax
import jax.numpy as jnp
from jax import lax
from jax.experimental import pallas as pl
from jax.experimental.pallas import tpu as pltpu
from jax.sharding import PartitionSpec as P

HEADS = 16
HDIM = 128
E = 448
SPAN = 64
NB = 128
NY = 4
NZ = 8
NX = 4
LOW = 208
TOP = 448 - LOW
LOW2 = 272
TOP2 = 448 - LOW2
MIB = 1024 * 1024
VMEM_ASK = 63 * MIB
MESH = pl.DeviceIdType.MESH
VM = pl.BlockSpec(memory_space=pltpu.VMEM)
SM = pl.BlockSpec(memory_space=pltpu.SMEM)


def places():
    s, b = lax.axis_index("seq"), lax.axis_index("batch")
    y, z = s // NZ, s % NZ
    x, c = b // 2, b % 2

    def at(dy, dz):
        return {"seq": ((y + dy + NY) % NY) * NZ + (z + dz + NZ) % NZ}

    dev = {
        "Y+": at(1, 0), "Y-": at(-1, 0), "YO": at(2, 0), "Z+": at(0, 1), "Z-": at(0, -1),
        "X+": {"batch": ((x + 1) % NX) * 2 + c},
        "X-": {"batch": ((x + NX - 1) % NX) * 2 + c},
        "C": {"batch": x * 2 + (1 - c)},
    }
    return y, z, x, c, dev


class Link:
    def __init__(self, dev, ssem, rsem):
        self.dev, self.ssem, self.rsem, self.n, self.kinds, self.sent = dev, ssem, rsem, 0, {}, {}

    def group(self):
        self.n += 1
        return self.n - 1

    def send(self, src, dst, to, kind, group=None):
        at = self.kinds.setdefault(kind, len(self.kinds))
        self.sent[kind] = self.sent.get(kind, 0) + math.prod(src.shape)
        cp = pltpu.make_async_remote_copy(
            src_ref=src, dst_ref=dst, send_sem=self.ssem.at[at],
            recv_sem=self.rsem.at[self.group() if group is None else group],
            device_id=self.dev[to], device_id_type=MESH,
        )
        cp.start()
        return cp

    def landed(self, ref, group):
        pltpu.make_async_copy(ref, ref, self.rsem.at[group]).wait()

    def gone(self, ref, kind):
        assert math.prod(ref.shape) == self.sent.pop(kind), kind
        pltpu.make_async_copy(ref, ref, self.ssem.at[self.kinds[kind]]).wait()


def barrier(dev, names):
    sem = pltpu.get_barrier_semaphore()
    for n in names:
        pl.semaphore_signal(sem, inc=1, device_id=dev[n], device_id_type=MESH)
    pl.semaphore_wait(sem, len(names))


def nt(a, b):
    return lax.dot_general(a, b, (((1,), (1,)), ((), ())), preferred_element_type=jnp.float32)


def tn(a, b):
    return lax.dot_general(a, b, (((0,), (0,)), ((), ())), preferred_element_type=jnp.float32)


N_LANDING = 93
N_LEAVING = 10


def body(place, near, pool, kw, vw, q_hbm, do_hbm, bias_hbm, att_hbm, qg_hbm, out,
         asm, inv, tab, wpad, q, do, bias, bias_t, wall, perm, wk, wv, qo, pp, r, tabs, stab, F, O, sb, sbo, rg,
         yr, yro, yso, acc, oc, zr, zo, of, ssem, rsem, lsem):
    y, z, x, c, dev = places()
    bf, f32 = jnp.bfloat16, jnp.float32
    scale = 1.0 / math.sqrt(HDIM)
    spans = r.shape[0]
    rows = spans * SPAN
    loads = [
        pltpu.make_async_copy(a, b, lsem.at[i])
        for i, (a, b) in enumerate(((bias_hbm, bias), (q_hbm, q), (do_hbm, do)))
    ]
    for cp in loads:
        cp.start()
    for j in range(2):
        F[j] = pool[j]
    mine = pl.ds(pl.multiple_of((2 * x + c) * 256, 256), 256)
    for k, w in enumerate((kw, vw)):
        wpad[...] = jnp.zeros_like(wpad)
        wpad[0:14] = w[:, mine].astype(f32)
        wall[0, 0, 0, 0, k] = wpad[...].astype(bf)
    reads = []
    down = lax.broadcasted_iota(jnp.int32, (8, 128), 0)
    along = lax.broadcasted_iota(jnp.int32, (8, 128), 1)
    wish = jnp.zeros((8, 128), jnp.int32)
    for i in range(spans):
        for j in range(2):
            pos = place[near[j, i]]
            owner, which = pos >> 1, pos & 1
            oy, oz = owner >> 3, owner & 7
            wish = jnp.where((down == oy) & (along == oz), which, wish)
            dy, dz = (y - oy) & 3, (z - oz) & 7
            far = jnp.where(dy == 1, 16, jnp.where(dy == 3, 24, 32)) + dz
            asm[2 * i + j] = jnp.where(dy == 0, 2 * dz + which, far)
            reads.append((dy * NZ + dz, which))
    tab[...] = wish
    barrier(dev, ["Y+", "Y-", "YO", "Z+", "Z-", "X+", "X-", "C"])
    L = Link(dev, ssem, rsem)

    def got(cps):
        for cp in cps:
            cp.wait_recv()

    tcp = [
        L.send(tab, tabs.at[k], to, "tab") for k, to in enumerate(("Y+", "Y-", "YO"))
    ]
    w1 = [
        L.send(wall.at[0, 0, 0, 0], wall.at[0, 0, 0, k], to, "w1")
        for k, to in ((1, "Y+"), (3, "Y-"), (2, "YO"))
    ]

    def own(k, j):
        a, b = k - 1, (NZ - k + 1) % NZ
        cps = []
        if k < 4 or j == 0:
            cps.append(L.send(F.at[2 * a + j], F.at[2 * k + j], "Z+", "block"))
        if k < 4 or j == 1:
            cps.append(L.send(F.at[2 * b + j], F.at[2 * (NZ - k) + j], "Z-", "block"))
        return cps

    def opp(k):
        a, b, m = k - 1, (NZ - k + 1) % NZ, NZ - k
        if k == 4:
            return [L.send(O.at[6], O.at[8], "Z+", "low"), L.send(O.at[11], O.at[9], "Z-", "low")]
        return [
            L.send(O.at[pl.ds(2 * a, 2)], O.at[pl.ds(2 * k, 2)], "Z+", "low"),
            L.send(O.at[pl.ds(2 * b, 2)], O.at[pl.ds(2 * m, 2)], "Z-", "low"),
        ]

    def weights(k):
        if k == 4:
            return [
                L.send(wall.at[0, 0, 5, pl.ds(0, 2)], wall.at[0, 0, 7, pl.ds(0, 2)], "Z+", "wz"),
                L.send(wall.at[0, 0, 6, pl.ds(2, 2)], wall.at[0, 0, 7, pl.ds(2, 2)], "Z-", "wz"),
            ]
        a, b = (0, 0) if k == 1 else (2 * k - 3, 2 * k - 2)
        return [
            L.send(wall.at[0, 0, a], wall.at[0, 0, 2 * k - 1], "Z+", "wz"),
            L.send(wall.at[0, 0, b], wall.at[0, 0, 2 * k], "Z-", "wz"),
        ]

    xs = {}
    to_core = [L.group() for _ in range(NX)]
    xf = L.group()

    def pieces(k):
        return pl.ds(0, 1) if k == 0 else pl.ds(7, 1) if k == 4 else pl.ds(2 * k - 1, 2)

    def core(dx, at):
        L.send(wall.at[dx, 0, at], wall.at[dx, 1, at], "C", "core", to_core[dx])

    def across(k):
        at = pieces(k)
        xs[k] = (
            L.send(wall.at[0, 0, at], wall.at[1, 0, at], "X+", "x"),
            L.send(wall.at[0, 0, at], wall.at[3, 0, at], "X-", "x"),
        )
        core(0, at)

    def across_on(k):
        got(xs[k])
        if k < 4:
            at = max(2 * k - 1, 0)
            L.send(wall.at[1, 0, at], wall.at[2, 0, at], "X+", "xf", xf)
        if k > 0:
            at = min(2 * k, 7)
            L.send(wall.at[3, 0, at], wall.at[2, 0, at], "X-", "xf", xf)
        core(1, pieces(k))
        core(3, pieces(k))

    direct, direct_top = L.group(), L.group()

    def ysend(d):
        zp = (z - d + NZ) % NZ
        sb[2 * d] = lax.select(stab[1, y, zp] > 0, F[2 * d + 1], F[2 * d])
        L.send(sb.at[2 * d], F.at[16 + d], "Y+", "block", direct)
        sb[2 * d + 1] = lax.select(stab[0, y, zp] > 0, F[2 * d + 1], F[2 * d])
        L.send(sb.at[2 * d + 1], F.at[24 + d], "Y-", "block", direct)
        sbo[d] = lax.select(stab[2, y, zp] > 0, F[2 * d + 1, 0:TOP], F[2 * d, 0:TOP])
        L.send(sbo.at[d], F.at[32 + d, pl.ds(0, TOP)], "YO", "top", direct_top)

    def project(dx, cc):
        if cc:
            L.landed(wall.at[dx, 1], to_core[dx])
        b = ((x - dx + NX) % NX) * 2 + (c + cc) % 2
        wide = pl.ds(pl.multiple_of(b * 256, 256), 256)
        pm = perm[...]
        for kv, w, src, base in ((0, wk, q, 0), (1, wv, do, HEADS * SPAN)):
            part = wall[dx, cc, :, :, kv].reshape(512, 256)
            wb = jnp.dot(pm, part, preferred_element_type=f32).astype(bf)
            w[:, wide] = wb
            rows_in = src[:, wide]
            for hh in range(2):
                t = nt(rows_in[:, hh * HDIM:(hh + 1) * HDIM], wb[:, hh * HDIM:(hh + 1) * HDIM])
                if kv == 0:
                    t = t * scale
                at = pl.ds(pl.multiple_of(base + b * 128 + hh * SPAN, SPAN), SPAN)
                qo[:, at] = t.astype(bf).reshape(spans, SPAN, E)

    o1 = [own(1, 0)]
    ex = L.send(F.at[pl.ds(0, 2), pl.ds(TOP, LOW)], O.at[pl.ds(0, 2)], "YO", "ex")
    got(w1)
    wz = weights(1)
    o1.append(own(1, 1))
    across(0)
    got(tcp)
    lc = [pltpu.make_async_copy(tabs.at[k], stab.at[k], lsem.at[3 + k]) for k in range(3)]
    for cp in lc:
        cp.start()
    for cp in lc:
        cp.wait()
    ysend(0)
    got(wz)
    wz = weights(2)
    got(o1[0])
    o2 = [own(2, 0)]
    got(o1[1])
    o2.append(own(2, 1))
    ysend(1)
    ysend(7)
    across(1)
    got(wz)
    wz = weights(3)
    got([ex])
    oz = opp(1)
    across_on(0)
    across(2)
    loads[0].wait()
    bias_t[...] = bias[...].T
    got(o2[0])
    o3 = [own(3, 0)]

    def find(k, _):
        read, which = jnp.int32(len(reads)), jnp.int32(0)
        for n, (owner, w) in enumerate(reads):
            read = jnp.where(owner == k, n, read)
            which = jnp.where(owner == k, w, which)
        inv[k] = read
        inv[32 + k] = which
        return 0

    lax.fori_loop(0, 32, find, 0)
    col = lax.broadcasted_iota(jnp.int32, (E, 512), 1)
    row = lax.broadcasted_iota(jnp.int32, (E, 512), 0)
    slot, dy, t = col >> 6, (col >> 4) & 3, col & 15
    dz = jnp.where((slot & 1) > 0, (slot + 1) >> 1, -((slot + 1) >> 1))
    source = (((y - dy) & 3) * NZ + ((z - dz) & 7)) * 14 + t
    perm[...] = jnp.where((source == row) & (t < 14), 1.0, 0.0).astype(bf)
    got(o2[1])
    ysend(2)
    ysend(6)
    got(wz)
    wz = weights(4)
    o3.append(own(3, 1))
    across_on(1)
    across(3)
    got(oz)
    oz = opp(2)
    across_on(2)
    got(wz)
    across(4)
    loads[1].wait()
    loads[2].wait()
    got(o3[0])
    got(o3[1])
    o4 = own(4, 0) + own(4, 1)
    ysend(3)
    ysend(5)
    across_on(3)
    project(0, 0)
    got(oz)
    oz = opp(3)
    across_on(4)
    project(0, 1)
    project(1, 0)
    got(o4)
    ysend(4)
    project(3, 0)
    L.landed(wall.at[2, 0], xf)
    core(2, pl.ds(0, NZ))
    got(oz)
    oz = opp(4)
    project(1, 1)
    project(3, 1)
    project(2, 0)
    project(2, 1)
    got(oz)
    L.landed(F.at[pl.ds(16, 16)], direct)
    L.landed(F.at[pl.ds(32, 8), pl.ds(0, TOP)], direct_top)
    for d in range(NZ):
        F[32 + d, TOP:448] = lax.select(inv[48 + d] > 0, O[2 * d + 1], O[2 * d])
    for i in range(spans):
        for j in range(2):
            r[i, j * NB:(j + 1) * NB] = F[asm[2 * i + j]].T
    for ref, kind in (
        (tabs, "tab"), (wall.at[0, 0, 0, pl.ds(0, 3)], "w1"), (wall.at[0, 0, pl.ds(0, 7)], "wz"),
        (wall.at[pl.ds(0, 2), 0], "x"), (wall.at[0, 0], "xf"), (wall.at[:, 0], "core"),
        (F.at[pl.ds(0, 30)], "block"), (O.at[pl.ds(0, 14)], "low"), (sbo, "top"),
        (O.at[pl.ds(0, 2)], "ex"),
    ):
        L.gone(ref, kind)

    half = HEADS * SPAN

    def stage1(i):
        return nt(r[i], qo[i, 0:half]) + bias_t[...], nt(r[i], qo[i, half:])

    def stage2(i, s, pg):
        e = jnp.exp(s - jnp.max(s, axis=0, keepdims=True))
        p = e * (1.0 / jnp.sum(e, axis=0, keepdims=True))
        low = p.astype(bf)
        delta = jnp.sum(low.astype(f32) * pg, axis=0, keepdims=True)
        ds = (p * (pg - delta)).astype(bf)
        pp[i, :, 0:half] = ds
        pp[i, :, half:] = low
        return ds, low

    def stage3(i, ds, low):
        g = jnp.dot(ds, qo[i, 0:half], preferred_element_type=f32)
        g = (g + jnp.dot(low, qo[i, half:], preferred_element_type=f32)).astype(bf)
        rg[2 * i] = g[0:NB].T
        rg[2 * i + 1] = g[NB:].T

    ahead, behind = stage1(0), None
    for i in range(spans):
        later = stage1(i + 1) if i + 1 < spans else None
        now = stage2(i, *ahead)
        if behind is not None:
            stage3(i - 1, *behind)
        ahead, behind = later, now
    stage3(spans - 1, *behind)
    rg[2 * spans] = jnp.zeros((448, 128), bf)

    back = {}

    def yslots(d):
        sb[2 * d] = rg[inv[8 + d]]
        group = L.group()
        L.send(sb.at[2 * d], yr.at[2 * d + 1], "Y-", "block", group)
        sb[2 * d + 1] = rg[inv[24 + d]]
        L.send(sb.at[2 * d + 1], yr.at[2 * d], "Y+", "block", group)
        yso[d] = rg[inv[16 + d], 0:TOP2]
        back[d] = group, L.send(yso.at[d], yro.at[d], "YO", "top")

    def back_home(d):
        group, top = back[d]
        L.landed(yr.at[pl.ds(2 * d, 2)], group)
        top.wait_recv()

    def dense(d):
        v = rg[inv[16 + d], TOP2:448]
        s = inv[48 + d]
        zero = jnp.zeros_like(v)
        oc[2 * d] = lax.select(s > 0, zero, v)
        oc[2 * d + 1] = lax.select(s > 0, v, zero)

    def pick(terms, j):
        t = None
        for v, s in terms:
            v = v.astype(f32)
            zero = jnp.zeros_like(v)
            v = lax.select(s > 0, v, zero) if j else lax.select(s > 0, zero, v)
            t = v if t is None else t + v
        return t

    def row_sum(d, j):
        zp = (z - d + NZ) % NZ
        s0, s1, s2 = tabs_at(0, zp), tabs_at(1, zp), tabs_at(2, zp)
        mine = rg[inv[d]]
        near = [(mine, inv[32 + d]), (yr[2 * d], s0), (yr[2 * d + 1], s1)]
        top = [(v[0:TOP2], s) for v, s in near] + [(yro[d], s2)]
        return pick(top, j), pick([(v[TOP2:448], s) for v, s in near], j)

    def tabs_at(k, zp):
        return stab[k, y, zp]

    def add_block(d, j, extra):
        top, low = row_sum(d, j)
        for ref in extra:
            top = top + ref[0:TOP2].astype(f32)
            low = low + ref[TOP2:448].astype(f32)
        return top, low

    group = 4 * SPAN
    outs = []

    def mix(g, base):
        for i in range(spans):
            t = tn(pp[i, :, base + g * group:base + (g + 1) * group], r[i])
            qo[i, base + g * group:base + (g + 1) * group] = t.astype(bf)

    def emit(g, base, w, dst, hbm, k):
        for h in range(4 * g, 4 * g + 4):
            v = qo[:, base + h * SPAN:base + (h + 1) * SPAN].reshape(rows, E)
            t = jnp.dot(v, w[:, h * HDIM:(h + 1) * HDIM], preferred_element_type=f32)
            if k == 1:
                t = t * scale
            dst[:, h * HDIM:(h + 1) * HDIM] = t.astype(bf)
        cols = pl.ds(4 * g * HDIM, 4 * HDIM)
        cp = pltpu.make_async_copy(dst.at[:, cols], hbm.at[:, cols], lsem.at[6 + 2 * g + k])
        cp.start()
        outs.append(cp)

    tasks = []
    for g in range(4):
        tasks.append(functools.partial(mix, g, half))
        tasks.append(functools.partial(emit, g, half, wv, q, att_hbm, 0))
        tasks.append(functools.partial(mix, g, 0))
        tasks.append(functools.partial(emit, g, 0, wk, do, qg_hbm, 1))

    def work(n):
        for _ in range(n):
            if tasks:
                tasks.pop(0)()

    def add_to(ref, i, n, src, k):
        for a in range(n):
            ref[i + a] = (ref[i + a].astype(f32) + src[k + a].astype(f32)).astype(bf)

    yslots(4)
    dense(4)
    oz = [L.send(oc.at[8], zo.at[0], "Z-", "low"), L.send(oc.at[9], zo.at[7], "Z+", "low")]
    yslots(3)
    yslots(5)
    dense(3)
    dense(5)
    yslots(2)
    yslots(6)
    yslots(1)
    yslots(7)
    yslots(0)
    for d in (2, 6, 1, 7, 0):
        dense(d)

    def own_back(e, prev):
        if e == 4:
            back_home(4)
            cps = []
            for j, to, at in ((0, "Z-", 0), (1, "Z+", 7)):
                top, low = row_sum(4, j)
                acc[8 + j, 0:TOP2] = top.astype(bf)
                acc[8 + j, TOP2:448] = low.astype(bf)
                cps.append(L.send(acc.at[8 + j], zr.at[at], to, "block"))
            return cps
        f = NZ - e
        back_home(e)
        back_home(f)
        at = 1 + 2 * (3 - e)
        cps = []
        for j in range(2):
            for d, base, to in ((e, 0, "Z-"), (f, 7, "Z+")):
                extra = []
                if e == 3:
                    if (j == 0) == (base == 0):
                        prev[base // 7].wait_recv()
                        extra = [zr.at[base]]
                else:
                    prev[2 * j + base // 7].wait_recv()
                    extra = [zr.at[base + at - 2 + j]]
                top, low = add_block(d, j, extra)
                acc[2 * d + j, 0:TOP2] = top.astype(bf)
                acc[2 * d + j, TOP2:448] = low.astype(bf)
                cps.append(L.send(acc.at[2 * d + j], zr.at[base + at + j], to, "block"))
        return cps

    def opp_back(e):
        got(oz)
        f = NZ - e
        if e == 3:
            add_to(oc, 6, 1, zo, 0)
            add_to(oc, 11, 1, zo, 7)
        elif e > 0:
            add_to(oc, 2 * e, 2, zo, 1 + 2 * (2 - e))
            add_to(oc, 2 * f, 2, zo, 8 + 2 * (2 - e))
        else:
            for j in range(2):
                t = oc[j].astype(f32) + zo[5 + j].astype(f32) + zo[12 + j].astype(f32)
                oc[j] = t.astype(bf)
            return [L.send(oc.at[pl.ds(0, 2)], of, "YO", "ex")]
        at = 1 + 2 * (3 - e)
        return [
            L.send(oc.at[pl.ds(2 * e, 2)], zo.at[pl.ds(at, 2)], "Z-", "low"),
            L.send(oc.at[pl.ds(2 * f, 2)], zo.at[pl.ds(7 + at, 2)], "Z+", "low"),
        ]

    work(1)
    oz = opp_back(3)
    work(1)
    oy = own_back(4, None)
    work(2)
    oz = opp_back(2)
    work(2)
    oy = own_back(3, oy)
    work(2)
    oz = opp_back(1)
    work(3)
    oy = own_back(2, oy)
    work(2)
    oz = opp_back(0)
    work(2)
    oy = own_back(1, oy)
    work(16)
    back_home(0)
    for j in range(2):
        got(oy[2 * j:2 * j + 2])
        if j == 0:
            got(oz)
        top, low = add_block(0, j, [zr.at[5 + j], zr.at[12 + j]])
        low = low + of[j].astype(f32)
        out[j, 0:TOP2] = top
        out[j, TOP2:448] = low
    for cp in outs:
        cp.wait()
    for ref, kind in (
        (F.at[pl.ds(0, 30)], "block"), (zo, "low"), (yso, "top"), (of, "ex"),
    ):
        L.gone(ref, kind)


def call(place, near, pool, kw, vw, q, do, bias):
    bf, f32 = jnp.bfloat16, jnp.float32
    rows = q.shape[0]
    spans = rows // SPAN
    sizes = (
        16, 64, ((8, 128), jnp.int32), ((16, 256), f32),
        ((rows, 2048), bf), ((rows, 2048), bf),
        ((HEADS * SPAN, 256), f32), ((256, HEADS * SPAN), f32),
        ((NX, 2, NZ, NY, 2, 16, 256), bf), ((E, 512), bf),
        ((E, 2048), bf), ((E, 2048), bf),
        ((spans, 2 * HEADS * SPAN, E), bf), ((spans, 256, 2 * HEADS * SPAN), bf),
        ((spans, 256, E), bf), ((3, 8, 128), jnp.int32), None,
        ((40, 448, 128), bf), ((16, LOW, 128), bf),
        ((16, 448, 128), bf), ((8, TOP, 128), bf), ((2 * spans + 1, 448, 128), bf),
        ((16, 448, 128), bf), ((8, TOP2, 128), bf), ((8, TOP2, 128), bf),
        ((16, 448, 128), bf), ((16, LOW2, 128), bf),
        ((14, 448, 128), bf), ((14, LOW2, 128), bf), ((2, LOW2, 128), bf),
    )
    scratch = [
        pltpu.SMEM((3, 8, 128), jnp.int32) if s is None
        else pltpu.SMEM((s,), jnp.int32) if isinstance(s, int)
        else pltpu.VMEM(*s) for s in sizes
    ]
    scratch += [
        pltpu.SemaphoreType.DMA((N_LEAVING,)), pltpu.SemaphoreType.DMA((N_LANDING,)),
        pltpu.SemaphoreType.DMA((14,)),
    ]
    hbm = pl.BlockSpec(memory_space=pl.ANY)
    return pl.pallas_call(
        body,
        out_shape=(
            jax.ShapeDtypeStruct(q.shape, bf),
            jax.ShapeDtypeStruct(q.shape, bf),
            jax.ShapeDtypeStruct((2, E, NB), f32),
        ),
        in_specs=[SM, SM, VM, VM, VM, hbm, hbm, hbm],
        out_specs=(hbm, hbm, VM),
        scratch_shapes=scratch,
        compiler_params=pltpu.CompilerParams(
            collective_id=0, has_side_effects=True, vmem_limit_bytes=VMEM_ASK
        ),
        name="retro",
    )(place, near, pool, kw, vw, q, do, bias)


def hand_over(*refs):
    n = 4
    src, dst, mid, sem = refs[0:3], refs[3:6], refs[6:9], refs[9]
    ins, outs = [], []
    for k in range(n):
        for a, m, b in zip(src[0:2], mid[0:2], dst[0:2]):
            part = pl.ds(k * (a.shape[0] // n), a.shape[0] // n)
            i = len(ins)
            ins.append(pltpu.make_async_copy(a.at[part], m.at[part], sem.at[2 * i]))
            outs.append(pltpu.make_async_copy(m.at[part], b.at[part], sem.at[2 * i + 1]))
    ins.append(pltpu.make_async_copy(src[2], mid[2], sem.at[4 * n]))
    outs.append(pltpu.make_async_copy(mid[2], dst[2], sem.at[4 * n + 1]))
    for cp in ins:
        cp.start()
    for a, b in zip(ins, outs):
        a.wait()
        b.start()
    for cp in outs:
        cp.wait()


def hand_over_call(*arrays):
    hbm = pl.BlockSpec(memory_space=pl.ANY)
    return pl.pallas_call(
        hand_over,
        out_shape=tuple(jax.ShapeDtypeStruct(a.shape, a.dtype) for a in arrays),
        in_specs=[hbm] * 3,
        out_specs=(hbm,) * 3,
        scratch_shapes=[pltpu.VMEM(a.shape, a.dtype) for a in arrays]
        + [pltpu.SemaphoreType.DMA((18,))],
        compiler_params=pltpu.CompilerParams(vmem_limit_bytes=VMEM_ASK),
        name="handover",
    )(*arrays)


def on_device(queries, cotangent, pool, key_weight, value_weight, score_bias, neighbours, place):
    bias = score_bias.reshape(HEADS * SPAN, 2 * NB)
    att, qg, pg = hand_over_call(*call(
        place, neighbours.T, jnp.transpose(pool, (0, 2, 1)), key_weight, value_weight,
        queries, cotangent, bias,
    ))
    return att, qg, jnp.transpose(pg, (0, 2, 1))


def solution(mesh):
    both = ("batch", "seq")
    in_specs = (
        P(both, None), P(both, None), P(both, None, None), P("seq", None), P("seq", None),
        P(), P(both, None), P("batch"),
    )
    out_specs = (P(both, None), P(both, None), P(both, None, None))
    return jax.shard_map(
        on_device, mesh=mesh, in_specs=in_specs, out_specs=out_specs, check_vma=False
    )
```

```python
import functools
import math

import jax
import jax.numpy as jnp
from jax import lax
from jax.experimental import pallas as pl
from jax.experimental.pallas import tpu as pltpu
from jax.sharding import PartitionSpec as P

HEADS = 16
HDIM = 128
E = 448
SPAN = 64
NB = 128
NY = 4
NZ = 8
NX = 4
LOW = 176
TOP = 448 - LOW
LOW2 = 256
TOP2 = 448 - LOW2
MIB = 1024 * 1024
VMEM_ASK = 63 * MIB
MESH = pl.DeviceIdType.MESH
VM = pl.BlockSpec(memory_space=pltpu.VMEM)
SM = pl.BlockSpec(memory_space=pltpu.SMEM)


def places():
    s, b = lax.axis_index("seq"), lax.axis_index("batch")
    y, z = s // NZ, s % NZ
    x, c = b // 2, b % 2

    def at(dy, dz):
        return {"seq": ((y + dy + NY) % NY) * NZ + (z + dz + NZ) % NZ}

    dev = {
        "Y+": at(1, 0), "Y-": at(-1, 0), "YO": at(2, 0), "Z+": at(0, 1), "Z-": at(0, -1),
        "X+": {"batch": ((x + 1) % NX) * 2 + c},
        "X-": {"batch": ((x + NX - 1) % NX) * 2 + c},
        "C": {"batch": x * 2 + (1 - c)},
    }
    return y, z, x, c, dev


class Link:
    def __init__(self, dev, ssem, rsem):
        self.dev, self.ssem, self.rsem, self.n, self.kinds, self.sent = dev, ssem, rsem, 0, {}, {}

    def group(self):
        self.n += 1
        return self.n - 1

    def send(self, src, dst, to, kind, group=None):
        at = self.kinds.setdefault(kind, len(self.kinds))
        self.sent[kind] = self.sent.get(kind, 0) + math.prod(src.shape)
        cp = pltpu.make_async_remote_copy(
            src_ref=src, dst_ref=dst, send_sem=self.ssem.at[at],
            recv_sem=self.rsem.at[self.group() if group is None else group],
            device_id=self.dev[to], device_id_type=MESH,
        )
        cp.start()
        return cp

    def landed(self, ref, group):
        pltpu.make_async_copy(ref, ref, self.rsem.at[group]).wait()

    def gone(self, ref, kind):
        assert math.prod(ref.shape) == self.sent.pop(kind), kind
        pltpu.make_async_copy(ref, ref, self.ssem.at[self.kinds[kind]]).wait()


def barrier(dev, names):
    sem = pltpu.get_barrier_semaphore()
    for n in names:
        pl.semaphore_signal(sem, inc=1, device_id=dev[n], device_id_type=MESH)
    pl.semaphore_wait(sem, len(names))


def nt(a, b):
    return lax.dot_general(a, b, (((1,), (1,)), ((), ())), preferred_element_type=jnp.float32)


def tn(a, b):
    return lax.dot_general(a, b, (((0,), (0,)), ((), ())), preferred_element_type=jnp.float32)


N_LANDING = 93
N_LEAVING = 10


def body(place, near, pool, kw, vw, q_hbm, do_hbm, bias_hbm, att_hbm, qg_hbm, out,
         asm, inv, tab, wpad, q, do, bias, bias_t, wall, perm, wk, wv, qo, pp, r, tabs, stab, F, O, sb, sbo, rg,
         yr, yro, yso, acc, oc, zr, zo, of, ssem, rsem, lsem):
    y, z, x, c, dev = places()
    bf, f32 = jnp.bfloat16, jnp.float32
    scale = 1.0 / math.sqrt(HDIM)
    spans = r.shape[0]
    rows = spans * SPAN
    loads = [
        pltpu.make_async_copy(a, b, lsem.at[i])
        for i, (a, b) in enumerate(((bias_hbm, bias), (q_hbm, q), (do_hbm, do)))
    ]
    for cp in loads:
        cp.start()
    for j in range(2):
        F[j] = pool[j]
    mine = pl.ds(pl.multiple_of((2 * x + c) * 256, 256), 256)
    for k, w in enumerate((kw, vw)):
        wpad[...] = jnp.zeros_like(wpad)
        wpad[0:14] = w[:, mine].astype(f32)
        wall[0, 0, 0, 0, k] = wpad[...].astype(bf)
    reads = []
    down = lax.broadcasted_iota(jnp.int32, (8, 128), 0)
    along = lax.broadcasted_iota(jnp.int32, (8, 128), 1)
    wish = jnp.zeros((8, 128), jnp.int32)
    for i in range(spans):
        for j in range(2):
            pos = place[near[j, i]]
            owner, which = pos >> 1, pos & 1
            oy, oz = owner >> 3, owner & 7
            wish = jnp.where((down == oy) & (along == oz), which, wish)
            dy, dz = (y - oy) & 3, (z - oz) & 7
            far = jnp.where(dy == 1, 16, jnp.where(dy == 3, 24, 32)) + dz
            asm[2 * i + j] = jnp.where(dy == 0, 2 * dz + which, far)
            reads.append((dy * NZ + dz, which))
    tab[...] = wish
    barrier(dev, ["Y+", "Y-", "YO", "Z+", "Z-", "X+", "X-", "C"])
    L = Link(dev, ssem, rsem)

    def got(cps):
        for cp in cps:
            cp.wait_recv()

    tcp = [
        L.send(tab, tabs.at[k], to, "tab") for k, to in enumerate(("Y+", "Y-", "YO"))
    ]
    w1 = [
        L.send(wall.at[0, 0, 0, 0], wall.at[0, 0, 0, k], to, "w1")
        for k, to in ((1, "Y+"), (3, "Y-"), (2, "YO"))
    ]

    def own(k, j):
        a, b = k - 1, (NZ - k + 1) % NZ
        cps = []
        if k < 4 or j == 0:
            cps.append(L.send(F.at[2 * a + j], F.at[2 * k + j], "Z+", "block"))
        if k < 4 or j == 1:
            cps.append(L.send(F.at[2 * b + j], F.at[2 * (NZ - k) + j], "Z-", "block"))
        return cps

    def opp(k):
        a, b, m = k - 1, (NZ - k + 1) % NZ, NZ - k
        if k == 4:
            return [L.send(O.at[6], O.at[8], "Z+", "low"), L.send(O.at[11], O.at[9], "Z-", "low")]
        return [
            L.send(O.at[pl.ds(2 * a, 2)], O.at[pl.ds(2 * k, 2)], "Z+", "low"),
            L.send(O.at[pl.ds(2 * b, 2)], O.at[pl.ds(2 * m, 2)], "Z-", "low"),
        ]

    def weights(k):
        if k == 4:
            return [
                L.send(wall.at[0, 0, 5, pl.ds(0, 2)], wall.at[0, 0, 7, pl.ds(0, 2)], "Z+", "wz"),
                L.send(wall.at[0, 0, 6, pl.ds(2, 2)], wall.at[0, 0, 7, pl.ds(2, 2)], "Z-", "wz"),
            ]
        a, b = (0, 0) if k == 1 else (2 * k - 3, 2 * k - 2)
        return [
            L.send(wall.at[0, 0, a], wall.at[0, 0, 2 * k - 1], "Z+", "wz"),
            L.send(wall.at[0, 0, b], wall.at[0, 0, 2 * k], "Z-", "wz"),
        ]

    xs = {}
    to_core = [L.group() for _ in range(NX)]
    xf = L.group()

    def pieces(k):
        return pl.ds(0, 1) if k == 0 else pl.ds(7, 1) if k == 4 else pl.ds(2 * k - 1, 2)

    def core(dx, at):
        L.send(wall.at[dx, 0, at], wall.at[dx, 1, at], "C", "core", to_core[dx])

    def across(k):
        at = pieces(k)
        xs[k] = (
            L.send(wall.at[0, 0, at], wall.at[1, 0, at], "X+", "x"),
            L.send(wall.at[0, 0, at], wall.at[3, 0, at], "X-", "x"),
        )
        core(0, at)

    def across_on(k):
        got(xs[k])
        if k < 4:
            at = max(2 * k - 1, 0)
            L.send(wall.at[1, 0, at], wall.at[2, 0, at], "X+", "xf", xf)
        if k > 0:
            at = min(2 * k, 7)
            L.send(wall.at[3, 0, at], wall.at[2, 0, at], "X-", "xf", xf)
        core(1, pieces(k))
        core(3, pieces(k))

    direct, direct_top = L.group(), L.group()

    def ysend(d):
        zp = (z - d + NZ) % NZ
        sb[2 * d] = lax.select(stab[1, y, zp] > 0, F[2 * d + 1], F[2 * d])
        L.send(sb.at[2 * d], F.at[16 + d], "Y+", "block", direct)
        sb[2 * d + 1] = lax.select(stab[0, y, zp] > 0, F[2 * d + 1], F[2 * d])
        L.send(sb.at[2 * d + 1], F.at[24 + d], "Y-", "block", direct)
        sbo[d] = lax.select(stab[2, y, zp] > 0, F[2 * d + 1, 0:TOP], F[2 * d, 0:TOP])
        L.send(sbo.at[d], F.at[32 + d, pl.ds(0, TOP)], "YO", "top", direct_top)

    def project(dx, cc):
        if cc:
            L.landed(wall.at[dx, 1], to_core[dx])
        b = ((x - dx + NX) % NX) * 2 + (c + cc) % 2
        wide = pl.ds(pl.multiple_of(b * 256, 256), 256)
        pm = perm[...]
        for kv, w, src, base in ((0, wk, q, 0), (1, wv, do, HEADS * SPAN)):
            part = wall[dx, cc, :, :, kv].reshape(512, 256)
            wb = jnp.dot(pm, part, preferred_element_type=f32).astype(bf)
            w[:, wide] = wb
            rows_in = src[:, wide]
            for hh in range(2):
                t = nt(rows_in[:, hh * HDIM:(hh + 1) * HDIM], wb[:, hh * HDIM:(hh + 1) * HDIM])
                if kv == 0:
                    t = t * scale
                at = pl.ds(pl.multiple_of(base + b * 128 + hh * SPAN, SPAN), SPAN)
                qo[:, at] = t.astype(bf).reshape(spans, SPAN, E)

    o1 = [own(1, 0)]
    ex = L.send(F.at[pl.ds(0, 2), pl.ds(TOP, LOW)], O.at[pl.ds(0, 2)], "YO", "ex")
    got(w1)
    wz = weights(1)
    o1.append(own(1, 1))
    across(0)
    got(tcp)
    lc = [pltpu.make_async_copy(tabs.at[k], stab.at[k], lsem.at[3 + k]) for k in range(3)]
    for cp in lc:
        cp.start()
    for cp in lc:
        cp.wait()
    ysend(0)
    got(wz)
    wz = weights(2)
    got(o1[0])
    o2 = [own(2, 0)]
    got(o1[1])
    o2.append(own(2, 1))
    ysend(1)
    ysend(7)
    across(1)
    got(wz)
    wz = weights(3)
    got([ex])
    oz = opp(1)
    across_on(0)
    across(2)
    loads[0].wait()
    bias_t[...] = bias[...].T
    got(o2[0])
    o3 = [own(3, 0)]

    def find(k, _):
        read, which = jnp.int32(len(reads)), jnp.int32(0)
        for n, (owner, w) in enumerate(reads):
            read = jnp.where(owner == k, n, read)
            which = jnp.where(owner == k, w, which)
        inv[k] = read
        inv[32 + k] = which
        return 0

    lax.fori_loop(0, 32, find, 0)
    col = lax.broadcasted_iota(jnp.int32, (E, 512), 1)
    row = lax.broadcasted_iota(jnp.int32, (E, 512), 0)
    slot, dy, t = col >> 6, (col >> 4) & 3, col & 15
    dz = jnp.where((slot & 1) > 0, (slot + 1) >> 1, -((slot + 1) >> 1))
    source = (((y - dy) & 3) * NZ + ((z - dz) & 7)) * 14 + t
    perm[...] = jnp.where((source == row) & (t < 14), 1.0, 0.0).astype(bf)
    got(o2[1])
    ysend(2)
    ysend(6)
    got(wz)
    wz = weights(4)
    o3.append(own(3, 1))
    across_on(1)
    across(3)
    got(oz)
    oz = opp(2)
    across_on(2)
    got(wz)
    across(4)
    loads[1].wait()
    loads[2].wait()
    got(o3[0])
    got(o3[1])
    o4 = own(4, 0) + own(4, 1)
    ysend(3)
    ysend(5)
    across_on(3)
    project(0, 0)
    got(oz)
    oz = opp(3)
    across_on(4)
    project(0, 1)
    project(1, 0)
    got(o4)
    ysend(4)
    project(3, 0)
    L.landed(wall.at[2, 0], xf)
    core(2, pl.ds(0, NZ))
    got(oz)
    oz = opp(4)
    project(1, 1)
    project(3, 1)
    project(2, 0)
    project(2, 1)
    got(oz)
    L.landed(F.at[pl.ds(16, 16)], direct)
    L.landed(F.at[pl.ds(32, 8), pl.ds(0, TOP)], direct_top)
    for d in range(NZ):
        F[32 + d, TOP:448] = lax.select(inv[48 + d] > 0, O[2 * d + 1], O[2 * d])
    for i in range(spans):
        for j in range(2):
            r[i, j * NB:(j + 1) * NB] = F[asm[2 * i + j]].T
    for ref, kind in (
        (tabs, "tab"), (wall.at[0, 0, 0, pl.ds(0, 3)], "w1"), (wall.at[0, 0, pl.ds(0, 7)], "wz"),
        (wall.at[pl.ds(0, 2), 0], "x"), (wall.at[0, 0], "xf"), (wall.at[:, 0], "core"),
        (F.at[pl.ds(0, 30)], "block"), (O.at[pl.ds(0, 14)], "low"), (sbo, "top"),
        (O.at[pl.ds(0, 2)], "ex"),
    ):
        L.gone(ref, kind)

    half = HEADS * SPAN

    def stage1(i):
        return nt(r[i], qo[i, 0:half]) + bias_t[...], nt(r[i], qo[i, half:])

    def stage2(i, s, pg):
        e = jnp.exp(s - jnp.max(s, axis=0, keepdims=True))
        p = e * (1.0 / jnp.sum(e, axis=0, keepdims=True))
        low = p.astype(bf)
        delta = jnp.sum(low.astype(f32) * pg, axis=0, keepdims=True)
        ds = (p * (pg - delta)).astype(bf)
        pp[i, :, 0:half] = ds
        pp[i, :, half:] = low
        return ds, low

    def stage3(i, ds, low, part):
        g = jnp.dot(ds, qo[i, 0:half, part], preferred_element_type=f32)
        g = (g + jnp.dot(low, qo[i, half:, part], preferred_element_type=f32)).astype(bf)
        rg[2 * i, part] = g[0:NB].T
        rg[2 * i + 1, part] = g[NB:].T

    first, second = slice(0, LOW2), slice(LOW2, 448)

    ahead, behind = stage1(0), None
    for i in range(spans):
        later = stage1(i + 1) if i + 1 < spans else None
        now = stage2(i, *ahead)
        if behind is not None:
            stage3(i - 1, *behind, first)
        ahead, behind = later, now
    stage3(spans - 1, *behind, first)
    rg[2 * spans] = jnp.zeros((448, 128), bf)

    back = {}

    def yslots(d, part):
        if d not in back:
            back[d] = L.group(), L.group()
        group, top = back[d]
        rows_at = pl.ds(part.start, part.stop - part.start)
        sb[2 * d, part] = rg[inv[8 + d], part]
        L.send(sb.at[2 * d, rows_at], yr.at[2 * d + 1, rows_at], "Y-", "block", group)
        sb[2 * d + 1, part] = rg[inv[24 + d], part]
        L.send(sb.at[2 * d + 1, rows_at], yr.at[2 * d, rows_at], "Y+", "block", group)
        if part.stop == 448:
            yso[d] = rg[inv[16 + d], second]
            L.send(yso.at[d], yro.at[d], "YO", "top", top)

    def back_home(d):
        group, top = back[d]
        L.landed(yr.at[pl.ds(2 * d, 2)], group)
        L.landed(yro.at[d], top)

    def dense(d):
        v = rg[inv[16 + d], first]
        s = inv[48 + d]
        zero = jnp.zeros_like(v)
        oc[2 * d] = lax.select(s > 0, zero, v)
        oc[2 * d + 1] = lax.select(s > 0, v, zero)

    def pick(terms, j):
        t = None
        for v, s in terms:
            v = v.astype(f32)
            zero = jnp.zeros_like(v)
            v = lax.select(s > 0, v, zero) if j else lax.select(s > 0, zero, v)
            t = v if t is None else t + v
        return t

    def row_sum(d, j):
        zp = (z - d + NZ) % NZ
        s0, s1, s2 = tabs_at(0, zp), tabs_at(1, zp), tabs_at(2, zp)
        mine = rg[inv[d]]
        near = [(mine, inv[32 + d]), (yr[2 * d], s0), (yr[2 * d + 1], s1)]
        top = [(v[second], s) for v, s in near] + [(yro[d], s2)]
        return pick(top, j), pick([(v[first], s) for v, s in near], j)

    def tabs_at(k, zp):
        return stab[k, y, zp]

    def add_block(d, j, extra):
        top, low = row_sum(d, j)
        for ref in extra:
            top = top + ref[second].astype(f32)
            low = low + ref[first].astype(f32)
        return top, low

    group = 4 * SPAN
    outs = []

    def mix(g, base):
        for i in range(spans):
            t = tn(pp[i, :, base + g * group:base + (g + 1) * group], r[i])
            qo[i, base + g * group:base + (g + 1) * group] = t.astype(bf)

    def emit(g, base, w, dst, hbm, k):
        for h in range(4 * g, 4 * g + 4):
            v = qo[:, base + h * SPAN:base + (h + 1) * SPAN].reshape(rows, E)
            t = jnp.dot(v, w[:, h * HDIM:(h + 1) * HDIM], preferred_element_type=f32)
            if k == 1:
                t = t * scale
            dst[:, h * HDIM:(h + 1) * HDIM] = t.astype(bf)
        cols = pl.ds(4 * g * HDIM, 4 * HDIM)
        cp = pltpu.make_async_copy(dst.at[:, cols], hbm.at[:, cols], lsem.at[6 + 2 * g + k])
        cp.start()
        outs.append(cp)

    tasks = []
    for g in range(4):
        tasks.append(functools.partial(mix, g, half))
        tasks.append(functools.partial(emit, g, half, wv, q, att_hbm, 0))
        tasks.append(functools.partial(mix, g, 0))
        tasks.append(functools.partial(emit, g, 0, wk, do, qg_hbm, 1))

    def work(n):
        for _ in range(n):
            if tasks:
                tasks.pop(0)()

    def add_to(ref, i, n, src, k):
        for a in range(n):
            ref[i + a] = (ref[i + a].astype(f32) + src[k + a].astype(f32)).astype(bf)

    yslots(4, first)
    dense(4)
    oz = [L.send(oc.at[8], zo.at[0], "Z-", "low"), L.send(oc.at[9], zo.at[7], "Z+", "low")]
    yslots(3, first)
    yslots(5, first)
    for i in range(spans):
        stage3(i, pp[i, :, 0:half], pp[i, :, half:], second)
    for d in (4, 3, 5):
        yslots(d, second)
    dense(3)
    dense(5)
    for d in (2, 6, 1, 7, 0):
        yslots(d, slice(0, 448))
    for d in (2, 6, 1, 7, 0):
        dense(d)

    def own_back(e, prev):
        if e == 4:
            back_home(4)
            cps = []
            for j, to, at in ((0, "Z-", 0), (1, "Z+", 7)):
                top, low = row_sum(4, j)
                acc[8 + j, second] = top.astype(bf)
                acc[8 + j, first] = low.astype(bf)
                cps.append(L.send(acc.at[8 + j], zr.at[at], to, "block"))
            return cps
        f = NZ - e
        back_home(e)
        back_home(f)
        at = 1 + 2 * (3 - e)
        cps = []
        for j in range(2):
            for d, base, to in ((e, 0, "Z-"), (f, 7, "Z+")):
                extra = []
                if e == 3:
                    if (j == 0) == (base == 0):
                        prev[base // 7].wait_recv()
                        extra = [zr.at[base]]
                else:
                    prev[2 * j + base // 7].wait_recv()
                    extra = [zr.at[base + at - 2 + j]]
                top, low = add_block(d, j, extra)
                acc[2 * d + j, second] = top.astype(bf)
                acc[2 * d + j, first] = low.astype(bf)
                cps.append(L.send(acc.at[2 * d + j], zr.at[base + at + j], to, "block"))
        return cps

    def opp_back(e):
        got(oz)
        f = NZ - e
        if e == 3:
            add_to(oc, 6, 1, zo, 0)
            add_to(oc, 11, 1, zo, 7)
        elif e > 0:
            add_to(oc, 2 * e, 2, zo, 1 + 2 * (2 - e))
            add_to(oc, 2 * f, 2, zo, 8 + 2 * (2 - e))
        else:
            for j in range(2):
                t = oc[j].astype(f32) + zo[5 + j].astype(f32) + zo[12 + j].astype(f32)
                oc[j] = t.astype(bf)
            return [L.send(oc.at[pl.ds(0, 2)], of, "YO", "ex")]
        at = 1 + 2 * (3 - e)
        return [
            L.send(oc.at[pl.ds(2 * e, 2)], zo.at[pl.ds(at, 2)], "Z-", "low"),
            L.send(oc.at[pl.ds(2 * f, 2)], zo.at[pl.ds(7 + at, 2)], "Z+", "low"),
        ]

    work(1)
    oz = opp_back(3)
    work(1)
    oy = own_back(4, None)
    work(2)
    oz = opp_back(2)
    work(2)
    oy = own_back(3, oy)
    work(2)
    oz = opp_back(1)
    work(3)
    oy = own_back(2, oy)
    work(2)
    oz = opp_back(0)
    work(2)
    oy = own_back(1, oy)
    work(16)
    back_home(0)
    for j in range(2):
        got(oy[2 * j:2 * j + 2])
        if j == 0:
            got(oz)
        top, low = add_block(0, j, [zr.at[5 + j], zr.at[12 + j]])
        low = low + of[j].astype(f32)
        out[j, second] = top
        out[j, first] = low
    for cp in outs:
        cp.wait()
    for ref, kind in (
        (F.at[pl.ds(0, 30)], "block"), (zo, "low"), (yso, "top"), (of, "ex"),
    ):
        L.gone(ref, kind)


def call(place, near, pool, kw, vw, q, do, bias):
    bf, f32 = jnp.bfloat16, jnp.float32
    rows = q.shape[0]
    spans = rows // SPAN
    sizes = (
        16, 64, ((8, 128), jnp.int32), ((16, 256), f32),
        ((rows, 2048), bf), ((rows, 2048), bf),
        ((HEADS * SPAN, 256), f32), ((256, HEADS * SPAN), f32),
        ((NX, 2, NZ, NY, 2, 16, 256), bf), ((E, 512), bf),
        ((E, 2048), bf), ((E, 2048), bf),
        ((spans, 2 * HEADS * SPAN, E), bf), ((spans, 256, 2 * HEADS * SPAN), bf),
        ((spans, 256, E), bf), ((3, 8, 128), jnp.int32), None,
        ((40, 448, 128), bf), ((16, LOW, 128), bf),
        ((16, 448, 128), bf), ((8, TOP, 128), bf), ((2 * spans + 1, 448, 128), bf),
        ((16, 448, 128), bf), ((8, TOP2, 128), bf), ((8, TOP2, 128), bf),
        ((16, 448, 128), bf), ((16, LOW2, 128), bf),
        ((14, 448, 128), bf), ((14, LOW2, 128), bf), ((2, LOW2, 128), bf),
    )
    scratch = [
        pltpu.SMEM((3, 8, 128), jnp.int32) if s is None
        else pltpu.SMEM((s,), jnp.int32) if isinstance(s, int)
        else pltpu.VMEM(*s) for s in sizes
    ]
    scratch += [
        pltpu.SemaphoreType.DMA((N_LEAVING,)), pltpu.SemaphoreType.DMA((N_LANDING,)),
        pltpu.SemaphoreType.DMA((14,)),
    ]
    hbm = pl.BlockSpec(memory_space=pl.ANY)
    return pl.pallas_call(
        body,
        out_shape=(
            jax.ShapeDtypeStruct(q.shape, bf),
            jax.ShapeDtypeStruct(q.shape, bf),
            jax.ShapeDtypeStruct((2, E, NB), f32),
        ),
        in_specs=[SM, SM, VM, VM, VM, hbm, hbm, hbm],
        out_specs=(hbm, hbm, VM),
        scratch_shapes=scratch,
        compiler_params=pltpu.CompilerParams(
            collective_id=0, has_side_effects=True, vmem_limit_bytes=VMEM_ASK
        ),
        name="retro",
    )(place, near, pool, kw, vw, q, do, bias)


def hand_over(*refs):
    n = 4
    src, dst, mid, sem = refs[0:3], refs[3:6], refs[6:9], refs[9]
    ins, outs = [], []
    for k in range(n):
        for a, m, b in zip(src[0:2], mid[0:2], dst[0:2]):
            part = pl.ds(k * (a.shape[0] // n), a.shape[0] // n)
            i = len(ins)
            ins.append(pltpu.make_async_copy(a.at[part], m.at[part], sem.at[2 * i]))
            outs.append(pltpu.make_async_copy(m.at[part], b.at[part], sem.at[2 * i + 1]))
    ins.append(pltpu.make_async_copy(src[2], mid[2], sem.at[4 * n]))
    outs.append(pltpu.make_async_copy(mid[2], dst[2], sem.at[4 * n + 1]))
    for cp in ins:
        cp.start()
    for a, b in zip(ins, outs):
        a.wait()
        b.start()
    for cp in outs:
        cp.wait()


def hand_over_call(*arrays):
    hbm = pl.BlockSpec(memory_space=pl.ANY)
    return pl.pallas_call(
        hand_over,
        out_shape=tuple(jax.ShapeDtypeStruct(a.shape, a.dtype) for a in arrays),
        in_specs=[hbm] * 3,
        out_specs=(hbm,) * 3,
        scratch_shapes=[pltpu.VMEM(a.shape, a.dtype) for a in arrays]
        + [pltpu.SemaphoreType.DMA((18,))],
        compiler_params=pltpu.CompilerParams(vmem_limit_bytes=VMEM_ASK),
        name="handover",
    )(*arrays)


def on_device(queries, cotangent, pool, key_weight, value_weight, score_bias, neighbours, place):
    bias = score_bias.reshape(HEADS * SPAN, 2 * NB)
    att, qg, pg = hand_over_call(*call(
        place, neighbours.T, jnp.transpose(pool, (0, 2, 1)), key_weight, value_weight,
        queries, cotangent, bias,
    ))
    return att, qg, jnp.transpose(pg, (0, 2, 1))


def solution(mesh):
    both = ("batch", "seq")
    in_specs = (
        P(both, None), P(both, None), P(both, None, None), P("seq", None), P("seq", None),
        P(), P(both, None), P("batch"),
    )
    out_specs = (P(both, None), P(both, None), P(both, None, None))
    return jax.shard_map(
        on_device, mesh=mesh, in_specs=in_specs, out_specs=out_specs, check_vma=False
    )
```

```python
import functools
import math

import jax
import jax.numpy as jnp
from jax import lax
from jax.experimental import pallas as pl
from jax.experimental.pallas import tpu as pltpu
from jax.sharding import PartitionSpec as P

HEADS = 16
HDIM = 128
E = 448
SPAN = 64
NB = 128
NY = 4
NZ = 8
NX = 4
LOW = 176
TOP = 448 - LOW
LOW2 = 256
TOP2 = 448 - LOW2
MIB = 1024 * 1024
VMEM_ASK = 63 * MIB
MESH = pl.DeviceIdType.MESH
VM = pl.BlockSpec(memory_space=pltpu.VMEM)
SM = pl.BlockSpec(memory_space=pltpu.SMEM)


def places():
    s, b = lax.axis_index("seq"), lax.axis_index("batch")
    y, z = s // NZ, s % NZ
    x, c = b // 2, b % 2

    def at(dy, dz):
        return {"seq": ((y + dy + NY) % NY) * NZ + (z + dz + NZ) % NZ}

    dev = {
        "Y+": at(1, 0), "Y-": at(-1, 0), "YO": at(2, 0), "Z+": at(0, 1), "Z-": at(0, -1),
        "X+": {"batch": ((x + 1) % NX) * 2 + c},
        "X-": {"batch": ((x + NX - 1) % NX) * 2 + c},
        "C": {"batch": x * 2 + (1 - c)},
    }
    return y, z, x, c, dev


class Link:
    def __init__(self, dev, ssem, rsem):
        self.dev, self.ssem, self.rsem, self.n, self.kinds, self.sent = dev, ssem, rsem, 0, {}, {}

    def group(self):
        self.n += 1
        return self.n - 1

    def send(self, src, dst, to, kind, group=None):
        at = self.kinds.setdefault(kind, len(self.kinds))
        self.sent[kind] = self.sent.get(kind, 0) + math.prod(src.shape)
        cp = pltpu.make_async_remote_copy(
            src_ref=src, dst_ref=dst, send_sem=self.ssem.at[at],
            recv_sem=self.rsem.at[self.group() if group is None else group],
            device_id=self.dev[to], device_id_type=MESH,
        )
        cp.start()
        return cp

    def landed(self, ref, group):
        pltpu.make_async_copy(ref, ref, self.rsem.at[group]).wait()

    def gone(self, ref, kind):
        assert math.prod(ref.shape) == self.sent.pop(kind), kind
        pltpu.make_async_copy(ref, ref, self.ssem.at[self.kinds[kind]]).wait()


def barrier(dev, names):
    sem = pltpu.get_barrier_semaphore()
    for n in names:
        pl.semaphore_signal(sem, inc=1, device_id=dev[n], device_id_type=MESH)
    return sem, len(names)


def nt(a, b):
    return lax.dot_general(a, b, (((1,), (1,)), ((), ())), preferred_element_type=jnp.float32)


def tn(a, b):
    return lax.dot_general(a, b, (((0,), (0,)), ((), ())), preferred_element_type=jnp.float32)


N_LANDING = 89
N_LEAVING = 10


def body(place, near, pool, kw, vw, q_hbm, do_hbm, bias_hbm, att_hbm, qg_hbm, out,
         asm, inv, tab, wpad, q, do, bias, bias_t, wall, perm, wk, wv, qo, pp, r, tabs, stab, F, O, sb, sbo, rg,
         yr, yro, yso, acc, oc, zr, zo, of, res, ssem, rsem, lsem):
    y, z, x, c, dev = places()
    bf, f32 = jnp.bfloat16, jnp.float32
    scale = 1.0 / math.sqrt(HDIM)
    spans = r.shape[0]
    rows = spans * SPAN
    met = barrier(dev, ["Y+", "Y-", "YO", "Z+", "Z-", "X+", "X-", "C"])
    loads = [
        pltpu.make_async_copy(a, b, lsem.at[i])
        for i, (a, b) in enumerate(((bias_hbm, bias), (q_hbm, q), (do_hbm, do)))
    ]
    for cp in loads:
        cp.start()
    for j in range(2):
        F[j] = pool[j]
    mine = pl.ds(pl.multiple_of((2 * x + c) * 256, 256), 256)
    for k, w in enumerate((kw, vw)):
        wpad[...] = jnp.zeros_like(wpad)
        wpad[0:14] = w[:, mine].astype(f32)
        wall[0, 0, 0, 0, k] = wpad[...].astype(bf)
    reads = []
    down = lax.broadcasted_iota(jnp.int32, (8, 128), 0)
    along = lax.broadcasted_iota(jnp.int32, (8, 128), 1)
    wish = jnp.zeros((8, 128), jnp.int32)
    for i in range(spans):
        for j in range(2):
            pos = place[near[j, i]]
            owner, which = pos >> 1, pos & 1
            oy, oz = owner >> 3, owner & 7
            wish = jnp.where((down == oy) & (along == oz), which, wish)
            dy, dz = (y - oy) & 3, (z - oz) & 7
            far = jnp.where(dy == 1, 16, jnp.where(dy == 3, 24, 32)) + dz
            asm[2 * i + j] = jnp.where(dy == 0, 2 * dz + which, far)
            reads.append((dy * NZ + dz, which))
    tab[...] = wish
    pl.semaphore_wait(*met)
    L = Link(dev, ssem, rsem)

    def got(cps):
        for cp in cps:
            cp.wait_recv()

    tg, wg = L.group(), L.group()
    tcp = [
        L.send(tab, tabs.at[k], to, "tab", tg) for k, to in enumerate(("Y+", "Y-", "YO"))
    ]
    w1 = [
        L.send(wall.at[0, 0, 0, 0], wall.at[0, 0, 0, k], to, "w1", wg)
        for k, to in ((1, "Y+"), (3, "Y-"), (2, "YO"))
    ]

    def own(k, j):
        a, b = k - 1, (NZ - k + 1) % NZ
        cps = []
        if k < 4 or j == 0:
            cps.append(L.send(F.at[2 * a + j], F.at[2 * k + j], "Z+", "block"))
        if k < 4 or j == 1:
            cps.append(L.send(F.at[2 * b + j], F.at[2 * (NZ - k) + j], "Z-", "block"))
        return cps

    def opp(k):
        a, b, m = k - 1, (NZ - k + 1) % NZ, NZ - k
        if k == 4:
            return [L.send(O.at[6], O.at[8], "Z+", "low"), L.send(O.at[11], O.at[9], "Z-", "low")]
        return [
            L.send(O.at[pl.ds(2 * a, 2)], O.at[pl.ds(2 * k, 2)], "Z+", "low"),
            L.send(O.at[pl.ds(2 * b, 2)], O.at[pl.ds(2 * m, 2)], "Z-", "low"),
        ]

    def weights(k):
        if k == 4:
            return [
                L.send(wall.at[0, 0, 5, pl.ds(0, 2)], wall.at[0, 0, 7, pl.ds(0, 2)], "Z+", "wz"),
                L.send(wall.at[0, 0, 6, pl.ds(2, 2)], wall.at[0, 0, 7, pl.ds(2, 2)], "Z-", "wz"),
            ]
        a, b = (0, 0) if k == 1 else (2 * k - 3, 2 * k - 2)
        return [
            L.send(wall.at[0, 0, a], wall.at[0, 0, 2 * k - 1], "Z+", "wz"),
            L.send(wall.at[0, 0, b], wall.at[0, 0, 2 * k], "Z-", "wz"),
        ]

    xs = {}
    to_core = [L.group() for _ in range(NX)]
    xf = L.group()

    def pieces(k):
        return pl.ds(0, 1) if k == 0 else pl.ds(7, 1) if k == 4 else pl.ds(2 * k - 1, 2)

    def core(dx, at):
        L.send(wall.at[dx, 0, at], wall.at[dx, 1, at], "C", "core", to_core[dx])

    def across(k):
        at = pieces(k)
        xs[k] = (
            L.send(wall.at[0, 0, at], wall.at[1, 0, at], "X+", "x"),
            L.send(wall.at[0, 0, at], wall.at[3, 0, at], "X-", "x"),
        )
        core(0, at)

    def across_on(k):
        got(xs[k])
        if k < 4:
            at = max(2 * k - 1, 0)
            L.send(wall.at[1, 0, at], wall.at[2, 0, at], "X+", "xf", xf)
        if k > 0:
            at = min(2 * k, 7)
            L.send(wall.at[3, 0, at], wall.at[2, 0, at], "X-", "xf", xf)
        core(1, pieces(k))
        core(3, pieces(k))

    direct, direct_top = L.group(), L.group()

    def ysend(d):
        zp = (z - d + NZ) % NZ
        sb[2 * d] = lax.select(stab[1, y, zp] > 0, F[2 * d + 1], F[2 * d])
        L.send(sb.at[2 * d], F.at[16 + d], "Y+", "block", direct)
        sb[2 * d + 1] = lax.select(stab[0, y, zp] > 0, F[2 * d + 1], F[2 * d])
        L.send(sb.at[2 * d + 1], F.at[24 + d], "Y-", "block", direct)
        sbo[d] = lax.select(stab[2, y, zp] > 0, F[2 * d + 1, 0:TOP], F[2 * d, 0:TOP])
        L.send(sbo.at[d], F.at[32 + d, pl.ds(0, TOP)], "YO", "top", direct_top)

    def project(dx, cc):
        if cc:
            L.landed(wall.at[dx, 1], to_core[dx])
        b = ((x - dx + NX) % NX) * 2 + (c + cc) % 2
        wide = pl.ds(pl.multiple_of(b * 256, 256), 256)
        pm = perm[...]
        for kv, w, src, base in ((0, wk, q, 0), (1, wv, do, HEADS * SPAN)):
            part = wall[dx, cc, :, :, kv].reshape(512, 256)
            wb = jnp.dot(pm, part, preferred_element_type=f32).astype(bf)
            w[:, wide] = wb
            rows_in = src[:, wide]
            for hh in range(2):
                t = nt(rows_in[:, hh * HDIM:(hh + 1) * HDIM], wb[:, hh * HDIM:(hh + 1) * HDIM])
                if kv == 0:
                    t = t * scale
                at = pl.ds(pl.multiple_of(base + b * 128 + hh * SPAN, SPAN), SPAN)
                qo[:, at] = t.astype(bf).reshape(spans, SPAN, E)

    o1 = [own(1, 0)]
    ex = L.send(F.at[pl.ds(0, 2), pl.ds(TOP, LOW)], O.at[pl.ds(0, 2)], "YO", "ex")
    L.landed(wall.at[0, 0, 0, pl.ds(1, 3)], wg)
    wz = weights(1)
    o1.append(own(1, 1))
    across(0)
    L.landed(tabs, tg)
    lc = [pltpu.make_async_copy(tabs.at[k], stab.at[k], lsem.at[3 + k]) for k in range(3)]
    for cp in lc:
        cp.start()
    for cp in lc:
        cp.wait()
    ysend(0)
    got(wz)
    wz = weights(2)
    got(o1[0])
    o2 = [own(2, 0)]
    got(o1[1])
    o2.append(own(2, 1))
    ysend(1)
    ysend(7)
    across(1)
    got(wz)
    wz = weights(3)
    got([ex])
    oz = opp(1)
    across_on(0)
    across(2)
    loads[0].wait()
    bias_t[...] = bias[...].T
    got(o2[0])
    o3 = [own(3, 0)]

    def find(k, _):
        read, which = jnp.int32(len(reads)), jnp.int32(0)
        for n, (owner, w) in enumerate(reads):
            read = jnp.where(owner == k, n, read)
            which = jnp.where(owner == k, w, which)
        inv[k] = read
        inv[32 + k] = which
        return 0

    lax.fori_loop(0, 32, find, 0)
    col = lax.broadcasted_iota(jnp.int32, (E, 512), 1)
    row = lax.broadcasted_iota(jnp.int32, (E, 512), 0)
    slot, dy, t = col >> 6, (col >> 4) & 3, col & 15
    dz = jnp.where((slot & 1) > 0, (slot + 1) >> 1, -((slot + 1) >> 1))
    source = (((y - dy) & 3) * NZ + ((z - dz) & 7)) * 14 + t
    perm[...] = jnp.where((source == row) & (t < 14), 1.0, 0.0).astype(bf)
    got(o2[1])
    ysend(2)
    ysend(6)
    got(wz)
    wz = weights(4)
    o3.append(own(3, 1))
    across_on(1)
    across(3)
    got(oz)
    oz = opp(2)
    across_on(2)
    got(wz)
    across(4)
    loads[1].wait()
    loads[2].wait()
    got(o3[0])
    got(o3[1])
    o4 = own(4, 0) + own(4, 1)
    ysend(3)
    ysend(5)
    across_on(3)
    project(0, 0)
    got(oz)
    oz = opp(3)
    across_on(4)
    project(0, 1)
    project(1, 0)
    got(o4)
    ysend(4)
    project(3, 0)
    L.landed(wall.at[2, 0], xf)
    core(2, pl.ds(0, NZ))
    got(oz)
    oz = opp(4)
    project(1, 1)
    project(3, 1)
    project(2, 0)
    project(2, 1)
    got(oz)
    L.landed(F.at[pl.ds(16, 16)], direct)
    L.landed(F.at[pl.ds(32, 8), pl.ds(0, TOP)], direct_top)
    for d in range(NZ):
        F[32 + d, TOP:448] = lax.select(inv[48 + d] > 0, O[2 * d + 1], O[2 * d])
    for i in range(spans):
        for j in range(2):
            r[i, j * NB:(j + 1) * NB] = F[asm[2 * i + j]].T
    for ref, kind in (
        (tabs, "tab"), (wall.at[0, 0, 0, pl.ds(0, 3)], "w1"), (wall.at[0, 0, pl.ds(0, 7)], "wz"),
        (wall.at[pl.ds(0, 2), 0], "x"), (wall.at[0, 0], "xf"), (wall.at[:, 0], "core"),
        (F.at[pl.ds(0, 30)], "block"), (O.at[pl.ds(0, 14)], "low"), (sbo, "top"),
        (O.at[pl.ds(0, 2)], "ex"),
    ):
        L.gone(ref, kind)

    half = HEADS * SPAN

    def stage1(i):
        return nt(r[i], qo[i, 0:half]) + bias_t[...], nt(r[i], qo[i, half:])

    def stage2(i, s, pg):
        e = jnp.exp(s - jnp.max(s, axis=0, keepdims=True))
        p = e * (1.0 / jnp.sum(e, axis=0, keepdims=True))
        low = p.astype(bf)
        delta = jnp.sum(low.astype(f32) * pg, axis=0, keepdims=True)
        ds = (p * (pg - delta)).astype(bf)
        pp[i, :, 0:half] = ds
        pp[i, :, half:] = low
        return ds, low

    def stage3(i, ds, low, part):
        g = jnp.dot(ds, qo[i, 0:half, part], preferred_element_type=f32)
        g = (g + jnp.dot(low, qo[i, half:, part], preferred_element_type=f32)).astype(bf)
        rg[2 * i, part] = g[0:NB].T
        rg[2 * i + 1, part] = g[NB:].T

    first, second = slice(0, LOW2), slice(LOW2, 448)

    ahead, behind = stage1(0), None
    for i in range(spans):
        later = stage1(i + 1) if i + 1 < spans else None
        now = stage2(i, *ahead)
        if behind is not None:
            stage3(i - 1, *behind, first)
        ahead, behind = later, now
    stage3(spans - 1, *behind, first)
    rg[2 * spans] = jnp.zeros((448, 128), bf)

    back = {}

    def yslots(d, part):
        if d not in back:
            back[d] = L.group(), L.group()
        group, top = back[d]
        rows_at = pl.ds(part.start, part.stop - part.start)
        sb[2 * d, part] = rg[inv[8 + d], part]
        L.send(sb.at[2 * d, rows_at], yr.at[2 * d + 1, rows_at], "Y-", "block", group)
        sb[2 * d + 1, part] = rg[inv[24 + d], part]
        L.send(sb.at[2 * d + 1, rows_at], yr.at[2 * d, rows_at], "Y+", "block", group)
        if part.stop == 448:
            yso[d] = rg[inv[16 + d], second]
            L.send(yso.at[d], yro.at[d], "YO", "top", top)

    def back_home(d):
        group, top = back[d]
        L.landed(yr.at[pl.ds(2 * d, 2)], group)
        L.landed(yro.at[d], top)

    def dense(d):
        v = rg[inv[16 + d], first]
        s = inv[48 + d]
        zero = jnp.zeros_like(v)
        oc[2 * d] = lax.select(s > 0, zero, v)
        oc[2 * d + 1] = lax.select(s > 0, v, zero)

    def pick(terms, j):
        t = None
        for v, s in terms:
            v = v.astype(f32)
            zero = jnp.zeros_like(v)
            v = lax.select(s > 0, v, zero) if j else lax.select(s > 0, zero, v)
            t = v if t is None else t + v
        return t

    def row_sum(d, j):
        zp = (z - d + NZ) % NZ
        s0, s1, s2 = tabs_at(0, zp), tabs_at(1, zp), tabs_at(2, zp)
        mine = rg[inv[d]]
        near = [(mine, inv[32 + d]), (yr[2 * d], s0), (yr[2 * d + 1], s1)]
        top = [(v[second], s) for v, s in near] + [(yro[d], s2)]
        return pick(top, j), pick([(v[first], s) for v, s in near], j)

    def tabs_at(k, zp):
        return stab[k, y, zp]

    def add_block(d, j, extra):
        top, low = row_sum(d, j)
        for ref in extra:
            top = top + ref[second].astype(f32)
            low = low + ref[first].astype(f32)
        return top, low

    group = 4 * SPAN
    outs = []

    def mix(g, base):
        for i in range(spans):
            t = tn(pp[i, :, base + g * group:base + (g + 1) * group], r[i])
            qo[i, base + g * group:base + (g + 1) * group] = t.astype(bf)

    def emit(g, base, w, dst, hbm, k):
        for h in range(4 * g, 4 * g + 4):
            v = qo[:, base + h * SPAN:base + (h + 1) * SPAN].reshape(rows, E)
            t = jnp.dot(v, w[:, h * HDIM:(h + 1) * HDIM], preferred_element_type=f32)
            if k == 1:
                t = t * scale
            dst[:, h * HDIM:(h + 1) * HDIM] = t.astype(bf)
        cols = pl.ds(4 * g * HDIM, 4 * HDIM)
        cp = pltpu.make_async_copy(dst.at[:, cols], hbm.at[:, cols], lsem.at[6 + 2 * g + k])
        cp.start()
        outs.append(cp)

    tasks = []
    for g in range(4):
        tasks.append(functools.partial(mix, g, half))
        tasks.append(functools.partial(emit, g, half, wv, q, att_hbm, 0))
        tasks.append(functools.partial(mix, g, 0))
        tasks.append(functools.partial(emit, g, 0, wk, do, qg_hbm, 1))

    def work(n):
        for _ in range(n):
            if tasks:
                tasks.pop(0)()

    def add_to(ref, i, n, src, k):
        for a in range(n):
            ref[i + a] = (ref[i + a].astype(f32) + src[k + a].astype(f32)).astype(bf)

    yslots(4, first)
    dense(4)
    oz = [L.send(oc.at[8], zo.at[0], "Z-", "low"), L.send(oc.at[9], zo.at[7], "Z+", "low")]
    yslots(3, first)
    yslots(5, first)
    for i in range(spans):
        stage3(i, pp[i, :, 0:half], pp[i, :, half:], second)
    for d in (4, 3, 5):
        yslots(d, second)
    dense(3)
    dense(5)
    for d in (2, 6, 1, 7, 0):
        yslots(d, slice(0, 448))
    for d in (2, 6, 1, 7, 0):
        dense(d)

    def own_back(e, prev):
        if e == 4:
            back_home(4)
            cps = []
            for j, to, at in ((0, "Z-", 0), (1, "Z+", 7)):
                top, low = row_sum(4, j)
                acc[8 + j, second] = top.astype(bf)
                acc[8 + j, first] = low.astype(bf)
                cps.append(L.send(acc.at[8 + j], zr.at[at], to, "block"))
            return cps
        f = NZ - e
        back_home(e)
        back_home(f)
        at = 1 + 2 * (3 - e)
        cps = []
        for j in range(2):
            for d, base, to in ((e, 0, "Z-"), (f, 7, "Z+")):
                extra = []
                if e == 3:
                    if (j == 0) == (base == 0):
                        prev[base // 7].wait_recv()
                        extra = [zr.at[base]]
                else:
                    prev[2 * j + base // 7].wait_recv()
                    extra = [zr.at[base + at - 2 + j]]
                top, low = add_block(d, j, extra)
                acc[2 * d + j, second] = top.astype(bf)
                acc[2 * d + j, first] = low.astype(bf)
                cps.append(L.send(acc.at[2 * d + j], zr.at[base + at + j], to, "block"))
        return cps

    def opp_back(e):
        got(oz)
        f = NZ - e
        if e == 3:
            add_to(oc, 6, 1, zo, 0)
            add_to(oc, 11, 1, zo, 7)
        elif e > 0:
            add_to(oc, 2 * e, 2, zo, 1 + 2 * (2 - e))
            add_to(oc, 2 * f, 2, zo, 8 + 2 * (2 - e))
        else:
            for j in range(2):
                t = oc[j].astype(f32) + zo[5 + j].astype(f32) + zo[12 + j].astype(f32)
                oc[j] = t.astype(bf)
            return [L.send(oc.at[pl.ds(0, 2)], of, "YO", "ex")]
        at = 1 + 2 * (3 - e)
        return [
            L.send(oc.at[pl.ds(2 * e, 2)], zo.at[pl.ds(at, 2)], "Z-", "low"),
            L.send(oc.at[pl.ds(2 * f, 2)], zo.at[pl.ds(7 + at, 2)], "Z+", "low"),
        ]

    work(1)
    oz = opp_back(3)
    work(1)
    oy = own_back(4, None)
    work(2)
    oz = opp_back(2)
    work(2)
    oy = own_back(3, oy)
    work(2)
    oz = opp_back(1)
    work(3)
    oy = own_back(2, oy)
    work(2)
    oz = opp_back(0)
    work(2)
    oy = own_back(1, oy)
    work(16)
    back_home(0)
    for j in range(2):
        got(oy[2 * j:2 * j + 2])
        if j == 0:
            got(oz)
        top, low = add_block(0, j, [zr.at[5 + j], zr.at[12 + j]])
        low = low + of[j].astype(f32)
        res[j, second] = top
        res[j, first] = low
        cp = pltpu.make_async_copy(res.at[j], out.at[j], lsem.at[14 + j])
        cp.start()
        outs.append(cp)
    for cp in outs:
        cp.wait()
    for ref, kind in (
        (F.at[pl.ds(0, 30)], "block"), (zo, "low"), (yso, "top"), (of, "ex"),
    ):
        L.gone(ref, kind)


def call(place, near, pool, kw, vw, q, do, bias):
    bf, f32 = jnp.bfloat16, jnp.float32
    rows = q.shape[0]
    spans = rows // SPAN
    sizes = (
        16, 64, ((8, 128), jnp.int32), ((16, 256), f32),
        ((rows, 2048), bf), ((rows, 2048), bf),
        ((HEADS * SPAN, 256), f32), ((256, HEADS * SPAN), f32),
        ((NX, 2, NZ, NY, 2, 16, 256), bf), ((E, 512), bf),
        ((E, 2048), bf), ((E, 2048), bf),
        ((spans, 2 * HEADS * SPAN, E), bf), ((spans, 256, 2 * HEADS * SPAN), bf),
        ((spans, 256, E), bf), ((3, 8, 128), jnp.int32), None,
        ((40, 448, 128), bf), ((16, LOW, 128), bf),
        ((16, 448, 128), bf), ((8, TOP, 128), bf), ((2 * spans + 1, 448, 128), bf),
        ((16, 448, 128), bf), ((8, TOP2, 128), bf), ((8, TOP2, 128), bf),
        ((16, 448, 128), bf), ((16, LOW2, 128), bf),
        ((14, 448, 128), bf), ((14, LOW2, 128), bf), ((2, LOW2, 128), bf),
        ((2, E, NB), f32),
    )
    scratch = [
        pltpu.SMEM((3, 8, 128), jnp.int32) if s is None
        else pltpu.SMEM((s,), jnp.int32) if isinstance(s, int)
        else pltpu.VMEM(*s) for s in sizes
    ]
    scratch += [
        pltpu.SemaphoreType.DMA((N_LEAVING,)), pltpu.SemaphoreType.DMA((N_LANDING,)),
        pltpu.SemaphoreType.DMA((16,)),
    ]
    hbm = pl.BlockSpec(memory_space=pl.ANY)
    return pl.pallas_call(
        body,
        out_shape=(
            jax.ShapeDtypeStruct(q.shape, bf),
            jax.ShapeDtypeStruct(q.shape, bf),
            jax.ShapeDtypeStruct((2, E, NB), f32),
        ),
        in_specs=[SM, SM, VM, VM, VM, hbm, hbm, hbm],
        out_specs=(hbm, hbm, hbm),
        scratch_shapes=scratch,
        compiler_params=pltpu.CompilerParams(
            collective_id=0, has_side_effects=True, vmem_limit_bytes=VMEM_ASK
        ),
        name="retro",
    )(place, near, pool, kw, vw, q, do, bias)


def hand_over(*refs):
    n = 4
    src, dst, mid, sem = refs[0:3], refs[3:6], refs[6:9], refs[9]
    ins, outs = [], []
    for k in range(n):
        for a, m, b in zip(src[0:2], mid[0:2], dst[0:2]):
            part = pl.ds(k * (a.shape[0] // n), a.shape[0] // n)
            i = len(ins)
            ins.append(pltpu.make_async_copy(a.at[part], m.at[part], sem.at[2 * i]))
            outs.append(pltpu.make_async_copy(m.at[part], b.at[part], sem.at[2 * i + 1]))
    ins.append(pltpu.make_async_copy(src[2], mid[2], sem.at[4 * n]))
    outs.append(pltpu.make_async_copy(mid[2], dst[2], sem.at[4 * n + 1]))
    for cp in ins:
        cp.start()
    for a, b in zip(ins, outs):
        a.wait()
        b.start()
    for cp in outs:
        cp.wait()


def hand_over_call(*arrays):
    hbm = pl.BlockSpec(memory_space=pl.ANY)
    return pl.pallas_call(
        hand_over,
        out_shape=tuple(jax.ShapeDtypeStruct(a.shape, a.dtype) for a in arrays),
        in_specs=[hbm] * 3,
        out_specs=(hbm,) * 3,
        scratch_shapes=[pltpu.VMEM(a.shape, a.dtype) for a in arrays]
        + [pltpu.SemaphoreType.DMA((18,))],
        compiler_params=pltpu.CompilerParams(vmem_limit_bytes=VMEM_ASK),
        name="handover",
    )(*arrays)


def on_device(queries, cotangent, pool, key_weight, value_weight, score_bias, neighbours, place):
    bias = score_bias.reshape(HEADS * SPAN, 2 * NB)
    att, qg, pg = hand_over_call(*call(
        place, neighbours.T, jnp.transpose(pool, (0, 2, 1)), key_weight, value_weight,
        queries, cotangent, bias,
    ))
    return att, qg, jnp.transpose(pg, (0, 2, 1))


def solution(mesh):
    both = ("batch", "seq")
    in_specs = (
        P(both, None), P(both, None), P(both, None, None), P("seq", None), P("seq", None),
        P(), P(both, None), P("batch"),
    )
    out_specs = (P(both, None), P(both, None), P(both, None, None))
    return jax.shard_map(
        on_device, mesh=mesh, in_specs=in_specs, out_specs=out_specs, check_vma=False
    )
```
